256 devices in a mesh: cp: 64 (over y, x, z_lo, core), hp: 4 (over z_hi).
Axes of the slice: x: 4, y: 4, z: 8 (z_hi: 4, z_lo: 2; z = z_hi * 2 + z_lo), core: 2. Of those that a mesh axis runs over, the one named last changes fastest.
Arguments:
- queries: bfloat16 [49152, 2560], P(('cp', 'hp')), may hold values from -160 to 160
- keys: bfloat16 [49152, 2560], P(('cp', 'hp')), may hold values from -6 to 6
- values: bfloat16 [49152, 2560], P(('cp', 'hp')), may hold values from -6 to 6
- grad_out: bfloat16 [49152, 2560], P(('cp', 'hp')), may hold values from -6 to 6
- lambdas: float32 [20], replicated, may hold values from 0.2 to 0.8
- norm_gain: float32 [128], replicated, may hold values from 0.25 to 1.75
- doc_lengths: int32 [128], replicated, may hold values from 1 to 768, 49152 in all
Outputs:
- grad_queries: bfloat16 [49152, 2560], P(('cp', 'hp'))
- grad_keys: bfloat16 [49152, 2560], P(('cp', 'hp'))
- grad_values: bfloat16 [49152, 2560], P(('cp', 'hp'))
The draws below stay inside these ranges and needn't reach their ends.
Inputs may be any that keep to these rules, and one draw needn't show every extreme that they name: `doc_lengths`: the lengths sum to 49152; the longest is exactly 768.
All inputs are finite; a program needn't handle non-finite values.
Results may differ from the reference program's by a relative error of at most 0.019.
Values may be sent and summed in bfloat16 or wider, within the bound.
No kernel may reach another device: no remote copies, remote signals or barrier semaphores. Data moves between devices by JAX's collectives and lax.ppermute only.
A program may use at most 128 MiB of HBM per device.

```python
import math
import jax
import jax.numpy as jnp
import numpy as np
from jax import lax

HEADS = 20
HEAD_DIM = 128
BLOCK = 768
TOKENS = 49152
MAXDOC = 768
DOCS = 128


def draw_queries(key, part):
    key = jax.random.fold_in(key, 1)
    normal_key = jax.random.fold_in(key, 0)
    entries = jax.random.normal(normal_key, (TOKENS, HEADS * HEAD_DIM), jnp.float32)
    entries = jnp.clip(entries, -6.0, 6.0)
    return entries.astype(jnp.bfloat16)


def levels(rng, extent, shards, low, largest):
    factor_of = 1.0
    for dim, parts in shards:
        heights = jax.random.uniform(jax.random.fold_in(jax.random.fold_in(rng, 6), dim), (parts,), jnp.float32, low / len(shards), largest / len(shards))
        factor_of = factor_of * jnp.repeat(jnp.exp(heights), extent[dim] // parts).reshape((-1,) + (1,) * (len(extent) - 1 - dim))
    return factor_of


def split_up(count, total, most, lean):
    portions = [(1 << 20) // math.isqrt(grade ** lean) + 1 for grade in range(2, count + 1)]
    surplus, counts = total - most - (count - 1), [1] * (count - 1)
    while surplus > 0:
        free = [i for i in range(count - 1) if counts[i] < most]
        pool, left = sum([portions[i] for i in free]), surplus
        for i in free:
            addition = min(most - counts[i], max(1, left * portions[i] // pool), surplus)
            counts[i] = counts[i] + addition
            surplus = surplus - addition
    return np.array([most] + counts)


def uneven_parts(rng, number_of, total, limit, slope):
    if number_of == 2:
        one = jax.random.randint(rng, (), max(1, total - limit), min(limit, total - 1) + 1)
        return jnp.stack([one, total - one])
    tallies = jnp.asarray(split_up(number_of, total, limit, slope), jnp.int32)
    pairs = (number_of - 1) // 2
    giver, sink = tallies[1:1 + 2 * pairs:2], tallies[2:2 + 2 * pairs:2]
    room = jnp.minimum(giver - 1, limit - sink)
    passed = jax.random.randint(jax.random.fold_in(rng, 1), (pairs,), 0, 1 << 20) % (room + 1)
    tallies = tallies.at[1:1 + 2 * pairs:2].set(giver - passed).at[2:2 + 2 * pairs:2].set(sink + passed)
    return tallies[jax.random.permutation(jax.random.fold_in(rng, 2), number_of)]


def noise(key, extent, scale, reach, cuts=(), kind=jnp.bfloat16):
    values = jax.random.normal(key, extent, jnp.float32) * scale
    if len(cuts) > 0:
        values = levels(key, extent, cuts, -0.22, 0.18) * values
    return jnp.clip(values, min=-reach, max=reach).astype(kind)


def setup_inputs(seed: int = 0) -> dict:
    streams_of = jax.random.split(jax.random.key(seed), 8)
    queries = draw_queries(jax.random.fold_in(streams_of[7], 71), 0)
    keys = noise(streams_of[1], (TOKENS, HEADS * HEAD_DIM), 1.0, 6.0, ((0, 256),))
    values = noise(streams_of[2], (TOKENS, HEADS * HEAD_DIM), 1.0, 6.0, ((0, 256),))
    grad_out = noise(streams_of[3], (TOKENS, HEADS * HEAD_DIM), 1.0, 6.0, ((0, 256),))
    lambdas = jnp.clip(jax.random.uniform(streams_of[4], (HEADS,), jnp.float32, 0.2, 0.8), 0.2, 0.8)
    norm_gain = jnp.clip(1.0 + 0.15 * jax.random.normal(streams_of[5], (HEAD_DIM,), jnp.float32), 0.25, 1.75)
    doc_lengths = uneven_parts(streams_of[6], DOCS, TOKENS, MAXDOC, 2).astype(jnp.int32)
    return dict(queries=queries, keys=keys, values=values, grad_out=grad_out, lambdas=lambdas, norm_gain=norm_gain, doc_lengths=doc_lengths)


score_scale = 0.125
norm_epsilon = 1e-05
lambda_init = 0.8
masked_value = -1e+30

def masked_softmax(scores, live_mask):
    row_top = lax.optimization_barrier(jnp.max(jnp.where(live_mask, scores, masked_value), axis=1, keepdims=True))
    raised = jnp.where(live_mask, jnp.exp(scores - row_top), 0.0)
    row_total = lax.optimization_barrier(jnp.sum(raised, axis=1, keepdims=True))
    return raised / row_total

def head_grads(query_head, key_head, value_head, grad_head, lam_head, norm_gain, live_mask):
    score_one = jnp.dot(query_head[:, :64], key_head[:, :64].T, preferred_element_type=jnp.float32) * score_scale
    score_two = jnp.dot(query_head[:, 64:], key_head[:, 64:].T, preferred_element_type=jnp.float32) * score_scale
    prob_one = masked_softmax(score_one, live_mask)
    prob_two = masked_softmax(score_two, live_mask)
    prob_one_b = prob_one.astype(jnp.bfloat16)
    prob_two_b = prob_two.astype(jnp.bfloat16)
    out_one = jnp.dot(prob_one_b, value_head, preferred_element_type=jnp.float32)
    out_two = jnp.dot(prob_two_b, value_head, preferred_element_type=jnp.float32)
    attended = out_one - lam_head * out_two
    scaled_grad = grad_head.astype(jnp.float32) * norm_gain * (1.0 - lambda_init)
    inv_rms = lax.rsqrt(lax.optimization_barrier(jnp.mean(attended * attended, axis=1, keepdims=True)) + norm_epsilon)
    d_attended = inv_rms * scaled_grad - attended * (inv_rms * inv_rms * inv_rms) * lax.optimization_barrier(jnp.mean(attended * scaled_grad, axis=1, keepdims=True))
    d_attended_b = d_attended.astype(jnp.bfloat16)
    delta_one = lax.optimization_barrier(jnp.sum(d_attended * out_one, axis=1, keepdims=True))
    delta_two = -lam_head * lax.optimization_barrier(jnp.sum(d_attended * out_two, axis=1, keepdims=True))
    grad_probs = jnp.dot(d_attended_b, value_head.T, preferred_element_type=jnp.float32)
    grad_one_b = (prob_one * (grad_probs - delta_one)).astype(jnp.bfloat16)
    grad_two_b = (prob_two * (-lam_head * grad_probs - delta_two)).astype(jnp.bfloat16)
    grad_query = jnp.concatenate([jnp.dot(grad_one_b, key_head[:, :64], preferred_element_type=jnp.float32) * score_scale, jnp.dot(grad_two_b, key_head[:, 64:], preferred_element_type=jnp.float32) * score_scale], axis=1)
    grad_key = jnp.concatenate([jnp.dot(grad_one_b.T, query_head[:, :64], preferred_element_type=jnp.float32) * score_scale, jnp.dot(grad_two_b.T, query_head[:, 64:], preferred_element_type=jnp.float32) * score_scale], axis=1)
    grad_value = jnp.dot(prob_one_b.T, d_attended_b, preferred_element_type=jnp.float32) - lam_head * jnp.dot(prob_two_b.T, d_attended_b, preferred_element_type=jnp.float32)
    return (grad_query.astype(jnp.bfloat16), grad_key, grad_value)

def reference(queries, keys, values, grad_out, lambdas, norm_gain, doc_lengths):
    width = HEADS * 128
    span_rows = BLOCK
    lead_rows = jnp.zeros((span_rows, width), keys.dtype)
    padded_keys = jnp.concatenate([lead_rows, keys], axis=0)
    padded_values = jnp.concatenate([lead_rows, values], axis=0)
    doc_ends = jnp.cumsum(doc_lengths).astype(jnp.int32)

    def doc_of(places):
        return lax.optimization_barrier(jnp.sum((doc_ends[None, :] <= places[:, None]).astype(jnp.int32), axis=1))

    def to_heads(matrix):
        return matrix.reshape(matrix.shape[0], HEADS, 128).transpose(1, 0, 2)

    def from_heads(stack):
        return stack.transpose(1, 0, 2).reshape(stack.shape[1], width)

    def one_span(sums, index):
        start = (index * span_rows).astype(jnp.int32)
        query_rows = lax.dynamic_slice_in_dim(queries, start, span_rows, 0)
        grad_rows = lax.dynamic_slice_in_dim(grad_out, start, span_rows, 0)
        key_win = lax.dynamic_slice_in_dim(padded_keys, start, 2 * span_rows, 0)
        value_win = lax.dynamic_slice_in_dim(padded_values, start, 2 * span_rows, 0)
        query_pos = start + jnp.arange(span_rows, dtype=jnp.int32)
        window_pos = start - span_rows + jnp.arange(2 * span_rows, dtype=jnp.int32)
        live_mask = (doc_of(query_pos)[:, None] == doc_of(window_pos)[None, :]) & (window_pos[None, :] <= query_pos[:, None]) & (window_pos[None, :] >= 0)

        def one_head(items):
            return head_grads(items[0], items[1], items[2], items[3], items[4], norm_gain, live_mask)
        stacked = lax.map(one_head, (to_heads(query_rows), to_heads(key_win), to_heads(value_win), to_heads(grad_rows), lambdas))
        key_sums, value_sums = sums
        key_sums = lax.dynamic_update_slice_in_dim(key_sums, lax.dynamic_slice_in_dim(key_sums, start, 2 * span_rows, 0) + from_heads(stacked[1]), start, 0)
        value_sums = lax.dynamic_update_slice_in_dim(value_sums, lax.dynamic_slice_in_dim(value_sums, start, 2 * span_rows, 0) + from_heads(stacked[2]), start, 0)
        return ((key_sums, value_sums), from_heads(stacked[0]))
    empty = jnp.zeros((TOKENS + span_rows, width), jnp.float32)
    sums, query_stack = lax.scan(one_span, (empty, empty), jnp.arange(TOKENS // span_rows, dtype=jnp.int32))
    grad_queries = query_stack.reshape(TOKENS, width)
    return (grad_queries, sums[0][span_rows:].astype(jnp.bfloat16), sums[1][span_rows:].astype(jnp.bfloat16))
```

```python
import functools

import jax
import jax.numpy as jnp
import numpy as np
from jax import lax
from jax.experimental import pallas as pl
from jax.experimental.pallas import tpu as pltpu
from jax.sharding import PartitionSpec as P

HEAD_DIM = 128
GROUPS = 4
SPAN = 768
ROWS = 192
TILE = 256
DEVICES = 256
score_scale = 0.125
norm_epsilon = 1e-05
lambda_init = 0.8
masked_value = -1e30

STAGES = ((0,), (1,), (2,), (3,), (4,))
OFFSETS = ((0, 2, 4, 6), (1, 3, 5, 7))


def place_of(device):
    hp, cp = device % 4, device // 4
    core, z_lo, x, y = cp % 2, (cp // 2) % 2, (cp // 4) % 4, cp // 16
    return y, x, hp * 2 + z_lo, core


def device_at(y, x, z, core):
    z = z % 8
    return (((y % 4 * 4 + x % 4) * 2 + z % 2) * 2 + core) * 4 + z // 2


def group_at(z, sign):
    return z // 2 if z % 2 == 0 else ((z - sign) % 8) // 2


class Plan:
    def __init__(self, index):
        sign = 1 if index % 2 == 0 else -1
        self.out_routes = [[] for _ in range(4)]
        send_group = np.zeros((DEVICES, 4), np.int32)
        recv_block = np.zeros((DEVICES, 4), np.int32)
        chunk = np.zeros((DEVICES,), np.int32)
        group = np.zeros((DEVICES,), np.int32)
        worker = {}
        for d in range(DEVICES):
            y, x, z, core = place_of(d)
            flip = (x + index) % 2
            z_lo = (z % 2) ^ flip
            chunk[d] = ((y * 4 + x) * 2 + z_lo) * 2 + core
            group[d] = group_at(z, sign)
            worker[(chunk[d], group[d])] = d
            for k, off in enumerate(OFFSETS[flip]):
                send_group[d, k] = group_at((z + off) % 8, sign)
                recv_block[d, k] = ((z - off) % 8) // 2
                self.out_routes[k].append((d, device_at(y, x, z + off, core)))
        self.back_routes = [[(b, a) for a, b in route] for route in self.out_routes]
        self.halo_route = [(worker[(c - 1, g)], worker[(c, g)]) for c in range(1, 64) for g in range(4)]
        self.halo_back = [(b, a) for a, b in self.halo_route]
        self.table = np.concatenate(
            [send_group, recv_block, chunk[:, None], group[:, None]], axis=1
        ).astype(np.int32)


def pack_kernel(heads, slots, info, k_ref, v_ref, q_ref, g_ref, *rest):
    outs, sem = rest[:4], rest[4]
    copies = []
    for k in range(4):
        for h in range(heads):
            col = pl.multiple_of((slots[h] * GROUPS + info[k]) * HEAD_DIM, HEAD_DIM)
            for a, src in enumerate((k_ref, v_ref, q_ref, g_ref)):
                copy = pltpu.make_async_copy(
                    src.at[:, pl.ds(col, HEAD_DIM)], outs[k].at[h, a], sem.at[len(copies)]
                )
                copy.start()
                copies.append(copy)
    for copy in copies:
        copy.wait()


def pack(info, slots, arrays):
    heads = len(slots)
    any_spec = pl.BlockSpec(memory_space=pl.ANY)
    return pl.pallas_call(
        functools.partial(pack_kernel, heads, slots),
        out_shape=[jax.ShapeDtypeStruct((heads, 4, ROWS, HEAD_DIM), jnp.bfloat16)] * 4,
        in_specs=[pl.BlockSpec(memory_space=pltpu.SMEM)] + [any_spec] * 4,
        out_specs=[any_spec] * 4,
        scratch_shapes=[pltpu.SemaphoreType.DMA((heads * 16,))],
        compiler_params=pltpu.CompilerParams(vmem_limit_bytes=4 * 2**20),
        cost_estimate=pl.CostEstimate(flops=0, bytes_accessed=heads * 1600000, transcendentals=0),
        name="pack",
    )(info, *arrays)


def order_kernel(heads, info, r0, r1, r2, r3, out, sem):
    copies = []
    for k, src in enumerate((r0, r1, r2, r3)):
        row = pl.multiple_of(info[4 + k] * ROWS, ROWS)
        for h in range(heads):
            for a in range(2):
                copy = pltpu.make_async_copy(
                    src.at[h, a], out.at[h, a, pl.ds(row, ROWS)], sem.at[len(copies)]
                )
                copy.start()
                copies.append(copy)
    for copy in copies:
        copy.wait()


def order_halo(info, received):
    heads = received[0].shape[0]
    any_spec = pl.BlockSpec(memory_space=pl.ANY)
    return pl.pallas_call(
        functools.partial(order_kernel, heads),
        out_shape=jax.ShapeDtypeStruct((heads, 2, SPAN, HEAD_DIM), jnp.bfloat16),
        in_specs=[pl.BlockSpec(memory_space=pltpu.SMEM)] + [any_spec] * 4,
        out_specs=any_spec,
        scratch_shapes=[pltpu.SemaphoreType.DMA((heads * 8,))],
        compiler_params=pltpu.CompilerParams(vmem_limit_bytes=4 * 2**20),
        cost_estimate=pl.CostEstimate(flops=0, bytes_accessed=heads * 800000, transcendentals=0),
        name="order",
    )(info, *received)


def dot_nt(a, b):
    return lax.dot_general(a, b, (((1,), (1,)), ((), ())), preferred_element_type=jnp.float32)


def dot_tn(a, b):
    return lax.dot_general(a, b, (((0,), (0,)), ((), ())), preferred_element_type=jnp.float32)


def main_kernel(
    info, lams, gain_ref, starts_ref, r0, r1, r2, r3, prev_ref,
    dq_ref, own_ref, back_ref, q_s, g_s, k_w, v_w, dk_s, dv_s,
):
    head = pl.program_id(0)
    k_w[:SPAN] = prev_ref[0, 0]
    v_w[:SPAN] = prev_ref[0, 1]
    for k, src in enumerate((r0, r1, r2, r3)):
        row = pl.multiple_of(info[4 + k] * ROWS, ROWS)
        k_w[pl.ds(SPAN + row, ROWS)] = src[0, 0]
        v_w[pl.ds(SPAN + row, ROWS)] = src[0, 1]
        q_s[pl.ds(row, ROWS)] = src[0, 2]
        g_s[pl.ds(row, ROWS)] = src[0, 3]
    dk_s[...] = jnp.zeros_like(dk_s)
    dv_s[...] = jnp.zeros_like(dv_s)
    lam = lams[head]

    def tile(i, n):
        width = n * TILE
        row = pl.multiple_of(i * TILE, TILE)
        left = pl.multiple_of((4 + i - n) * TILE, TILE)
        rows, cols = pl.ds(row, TILE), pl.ds(left, width)
        k, v = k_w[cols], v_w[cols]
        first = lax.broadcasted_iota(jnp.int32, (TILE, HEAD_DIM), 1) < HEAD_DIM // 2
        q = (q_s[rows].astype(jnp.float32) * score_scale)
        q_two = jnp.concatenate(
            [jnp.where(first, q, 0.0), jnp.where(first, 0.0, q)], axis=0
        ).astype(jnp.bfloat16)
        scores = dot_nt(q_two, k)
        spot = lax.broadcasted_iota(jnp.int32, (TILE, width), 1) + left
        own = lax.broadcasted_iota(jnp.int32, (TILE, width), 0) + (row + SPAN)
        live = (spot >= starts_ref[rows]) & (spot <= own)

        def soft(score):
            score = jnp.where(live, score, masked_value)
            raised = jnp.exp(score - jnp.max(score, axis=1, keepdims=True))
            return raised * (1.0 / jnp.sum(raised, axis=1, keepdims=True))

        prob_one, prob_two = soft(scores[:TILE]), soft(scores[TILE:])
        prob_one_b, prob_two_b = prob_one.astype(jnp.bfloat16), prob_two.astype(jnp.bfloat16)
        out_one = jnp.dot(prob_one_b, v, preferred_element_type=jnp.float32)
        out_two = jnp.dot(prob_two_b, v, preferred_element_type=jnp.float32)
        attended = out_one - lam * out_two
        scaled = g_s[rows].astype(jnp.float32) * gain_ref[...] * (1.0 - lambda_init)
        inv_rms = lax.rsqrt(jnp.mean(attended * attended, axis=1, keepdims=True) + norm_epsilon)
        d_att = inv_rms * scaled - attended * (inv_rms * inv_rms * inv_rms) * jnp.mean(
            attended * scaled, axis=1, keepdims=True
        )
        d_att_b = d_att.astype(jnp.bfloat16)
        delta_one = jnp.sum(d_att * out_one, axis=1, keepdims=True)
        delta_two = -lam * jnp.sum(d_att * out_two, axis=1, keepdims=True)
        grad_probs = dot_nt(d_att_b, v)
        ds_one = (prob_one * (grad_probs - delta_one)).astype(jnp.bfloat16)
        ds_two = (prob_two * (-lam * grad_probs - delta_two)).astype(jnp.bfloat16)
        dq_one = jnp.dot(ds_one, k, preferred_element_type=jnp.float32)
        dq_two = jnp.dot(ds_two, k, preferred_element_type=jnp.float32)
        dq_ref[0, rows] = (jnp.where(first, dq_one, dq_two) * score_scale).astype(jnp.bfloat16)
        dk_s[cols] += dot_tn(ds_one, q_two[:TILE]) + dot_tn(ds_two, q_two[TILE:])
        dv_s[cols] += dot_tn(prob_one_b, d_att_b) - lam * dot_tn(prob_two_b, d_att_b)

    def step(i, carry):
        tiles = info[10 + i]
        for n in range(1, 5):
            pl.when(tiles == n)(functools.partial(tile, i, n))
        return carry

    lax.fori_loop(0, SPAN // TILE, step, 0)
    back_ref[0, 0] = dk_s[:SPAN].astype(jnp.bfloat16)
    back_ref[0, 1] = dv_s[:SPAN].astype(jnp.bfloat16)
    own_ref[0, 0] = dk_s[SPAN:]
    own_ref[0, 1] = dv_s[SPAN:]


def attend(info, lams, gain, starts, received, prev):
    heads = prev.shape[0]
    smem = pl.BlockSpec(memory_space=pltpu.SMEM)
    return pl.pallas_call(
        main_kernel,
        grid=(heads,),
        out_shape=[
            jax.ShapeDtypeStruct((heads, SPAN, HEAD_DIM), jnp.bfloat16),
            jax.ShapeDtypeStruct((heads, 2, SPAN, HEAD_DIM), jnp.float32),
            jax.ShapeDtypeStruct((heads, 2, SPAN, HEAD_DIM), jnp.bfloat16),
        ],
        in_specs=[
            smem,
            smem,
            pl.BlockSpec((1, HEAD_DIM), lambda h: (0, 0)),
            pl.BlockSpec((SPAN, 1), lambda h: (0, 0)),
        ]
        + [pl.BlockSpec((1, 4, ROWS, HEAD_DIM), lambda h: (h, 0, 0, 0))] * 4
        + [pl.BlockSpec((1, 2, SPAN, HEAD_DIM), lambda h: (h, 0, 0, 0))],
        out_specs=[
            pl.BlockSpec((1, SPAN, HEAD_DIM), lambda h: (h, 0, 0)),
            pl.BlockSpec((1, 2, SPAN, HEAD_DIM), lambda h: (h, 0, 0, 0)),
            pl.BlockSpec((1, 2, SPAN, HEAD_DIM), lambda h: (h, 0, 0, 0)),
        ],
        scratch_shapes=[
            pltpu.VMEM((SPAN, HEAD_DIM), jnp.bfloat16),
            pltpu.VMEM((SPAN, HEAD_DIM), jnp.bfloat16),
            pltpu.VMEM((2 * SPAN, HEAD_DIM), jnp.bfloat16),
            pltpu.VMEM((2 * SPAN, HEAD_DIM), jnp.bfloat16),
            pltpu.VMEM((2 * SPAN, HEAD_DIM), jnp.float32),
            pltpu.VMEM((2 * SPAN, HEAD_DIM), jnp.float32),
        ],
        compiler_params=pltpu.CompilerParams(vmem_limit_bytes=32 * 2**20),
        cost_estimate=pl.CostEstimate(
            flops=heads * 6 * 10**9, bytes_accessed=heads * 3 * 10**6, transcendentals=heads * 10**6
        ),
        name="attend",
    )(info, lams, gain, starts, *received, prev)


def merge_kernel(info, dq_ref, own_ref, halo_ref, *outs):
    for k, out in enumerate(outs):
        rows = pl.ds(pl.multiple_of(info[4 + k] * ROWS, ROWS), ROWS)
        out[0, 0] = dq_ref[0, rows]
        for a in range(2):
            out[0, 1 + a] = (own_ref[0, a, rows] + halo_ref[0, a, rows].astype(jnp.float32)).astype(
                jnp.bfloat16
            )


def merge(info, dq, own, halo):
    heads = dq.shape[0]
    return pl.pallas_call(
        merge_kernel,
        grid=(heads,),
        out_shape=[jax.ShapeDtypeStruct((heads, 3, ROWS, HEAD_DIM), jnp.bfloat16)] * 4,
        in_specs=[
            pl.BlockSpec(memory_space=pltpu.SMEM),
            pl.BlockSpec((1, SPAN, HEAD_DIM), lambda h: (h, 0, 0)),
            pl.BlockSpec((1, 2, SPAN, HEAD_DIM), lambda h: (h, 0, 0, 0)),
            pl.BlockSpec((1, 2, SPAN, HEAD_DIM), lambda h: (h, 0, 0, 0)),
        ],
        out_specs=[pl.BlockSpec((1, 3, ROWS, HEAD_DIM), lambda h: (h, 0, 0, 0))] * 4,
        compiler_params=pltpu.CompilerParams(vmem_limit_bytes=8 * 2**20),
        cost_estimate=pl.CostEstimate(flops=0, bytes_accessed=heads * 2000000, transcendentals=0),
        name="merge",
    )(info, dq, own, halo)


def unpack_kernel(heads_of, groups, *refs):
    count = sum(4 for _ in heads_of)
    srcs, outs, sem = refs[:count], refs[count:count + 3], refs[count + 3]
    copies = []
    for s, slots in enumerate(heads_of):
        for k in range(4):
            for h, slot in enumerate(slots):
                col = pl.multiple_of((slot * GROUPS + groups[s, k]) * HEAD_DIM, HEAD_DIM)
                for a in range(3):
                    copy = pltpu.make_async_copy(
                        srcs[s * 4 + k].at[h, a], outs[a].at[:, pl.ds(col, HEAD_DIM)],
                        sem.at[len(copies)],
                    )
                    copy.start()
                    copies.append(copy)
    for copy in copies:
        copy.wait()


def unpack(groups, heads_of, buffers, width):
    any_spec = pl.BlockSpec(memory_space=pl.ANY)
    return pl.pallas_call(
        functools.partial(unpack_kernel, heads_of),
        out_shape=[jax.ShapeDtypeStruct((ROWS, width), jnp.bfloat16)] * 3,
        in_specs=[pl.BlockSpec(memory_space=pltpu.SMEM)] + [any_spec] * len(buffers),
        out_specs=[any_spec] * 3,
        scratch_shapes=[pltpu.SemaphoreType.DMA((sum(map(len, heads_of)) * 12,))],
        compiler_params=pltpu.CompilerParams(vmem_limit_bytes=4 * 2**20),
        name="unpack",
    )(groups, *buffers)


def per_device(queries, keys, values, grad_out, lambdas, norm_gain, doc_lengths):
    axes = ("cp", "hp")
    me = lax.axis_index("cp") * lax.axis_size("hp") + lax.axis_index("hp")
    plans = [Plan(0), Plan(1)]
    doc_ends = jnp.cumsum(doc_lengths)
    tables, starts_of = [], []
    for plan in plans:
        line = jnp.asarray(plan.table)[me]
        at = line[8] * SPAN + jnp.arange(SPAN, dtype=jnp.int32)
        begin = jnp.max(
            jnp.where(doc_ends[None, :] <= at[:, None], doc_ends[None, :], 0), axis=1
        ) - (line[8] - 1) * SPAN
        tiles = 4 + jnp.arange(3, dtype=jnp.int32) - begin[::TILE] // TILE
        tables.append(jnp.concatenate([line, tiles]))
        starts_of.append(begin[:, None])
    gain = norm_gain[None, :]
    arrays = (keys, values, queries, grad_out)
    finals = []
    groups = []
    for index, slots in enumerate(STAGES):
        plan, info, starts = plans[index % 2], tables[index % 2], starts_of[index % 2]
        sent = pack(info, slots, arrays)
        received = [lax.ppermute(b, axes, route) for b, route in zip(sent, plan.out_routes)]
        prev = lax.ppermute(order_halo(info, received), axes, plan.halo_route)
        lams = jnp.stack([lambdas[slot * GROUPS + info[9]] for slot in slots])
        dq, own, back = attend(info, lams, gain, starts, received, prev)
        halo = lax.ppermute(back, axes, plan.halo_back)
        outs = merge(info, dq, own, halo)
        finals += [lax.ppermute(b, axes, route) for b, route in zip(outs, plan.back_routes)]
        groups.append(info[:4])
    return tuple(unpack(jnp.stack(groups), STAGES, finals, queries.shape[1]))


def solution(mesh):
    spec = P(("cp", "hp"), None)
    return jax.shard_map(
        per_device,
        mesh=mesh,
        in_specs=(spec,) * 4 + (P(),) * 3,
        out_specs=(spec,) * 3,
        check_vma=False,
    )
```

```python
import functools

import jax
import jax.numpy as jnp
import numpy as np
from jax import lax
from jax.experimental import pallas as pl
from jax.experimental.pallas import tpu as pltpu
from jax.sharding import PartitionSpec as P

HEAD_DIM = 128
GROUPS = 4
SPAN = 768
ROWS = 192
TILE = 256
DEVICES = 256
score_scale = 0.125
norm_epsilon = 1e-05
lambda_init = 0.8
masked_value = -1e30

STAGES = ((0,), (1,), (2,), (3,), (4,))
ORDER = (
    "P0",
    "P1",
    "P2",
    "O0",
    "A0",
    "P3<A0",
    "O1",
    "A1<A0",
    "P4<A1",
    "O2",
    "A2<A1",
    "O3",
    "A3<A2",
    "O4",
    "A4<A3",
    "M0",
    "M1",
    "M2",
    "M3",
    "M4<X0<X1",
)
OFFSETS = ((0, 2, 4, 6), (1, 3, 5, 7))


def place_of(device):
    hp, cp = device % 4, device // 4
    core, z_lo, x, y = cp % 2, (cp // 2) % 2, (cp // 4) % 4, cp // 16
    return y, x, hp * 2 + z_lo, core


def device_at(y, x, z, core):
    z = z % 8
    return (((y % 4 * 4 + x % 4) * 2 + z % 2) * 2 + core) * 4 + z // 2


def group_at(z, sign):
    return z // 2 if z % 2 == 0 else ((z - sign) % 8) // 2


class Plan:
    def __init__(self, index):
        sign = 1 if index % 2 == 0 else -1
        self.out_routes = [[] for _ in range(4)]
        send_group = np.zeros((DEVICES, 4), np.int32)
        recv_block = np.zeros((DEVICES, 4), np.int32)
        chunk = np.zeros((DEVICES,), np.int32)
        group = np.zeros((DEVICES,), np.int32)
        worker = {}
        for d in range(DEVICES):
            y, x, z, core = place_of(d)
            flip = (x + index) % 2
            z_lo = (z % 2) ^ flip
            chunk[d] = ((y * 4 + x) * 2 + z_lo) * 2 + core
            group[d] = group_at(z, sign)
            worker[(chunk[d], group[d])] = d
            for k, off in enumerate(OFFSETS[flip]):
                send_group[d, k] = group_at((z + off) % 8, sign)
                recv_block[d, k] = ((z - off) % 8) // 2
                self.out_routes[k].append((d, device_at(y, x, z + off, core)))
        self.back_routes = [[(b, a) for a, b in route] for route in self.out_routes]
        self.halo_route = [(worker[(c - 1, g)], worker[(c, g)]) for c in range(1, 64) for g in range(4)]
        self.halo_back = [(b, a) for a, b in self.halo_route]
        self.table = np.concatenate(
            [send_group, recv_block, chunk[:, None], group[:, None]], axis=1
        ).astype(np.int32)


def spread(kernel, inputs, deps):
    def ordered(*refs):
        kernel(*refs[:inputs], *refs[inputs + len(deps):])

    return ordered


any_spec = pl.BlockSpec(memory_space=pl.ANY)
hbm_spec = pl.BlockSpec(memory_space=pltpu.HBM)


def pack_kernel(heads, slots, info, k_ref, v_ref, q_ref, g_ref, *rest):
    outs, sem = rest[:4], rest[4]
    copies = []
    for k in range(4):
        for h in range(heads):
            col = pl.multiple_of((slots[h] * GROUPS + info[k]) * HEAD_DIM, HEAD_DIM)
            for a, src in enumerate((k_ref, v_ref, q_ref, g_ref)):
                copy = pltpu.make_async_copy(
                    src.at[:, pl.ds(col, HEAD_DIM)], outs[k].at[h, a], sem.at[len(copies)]
                )
                copy.start()
                copies.append(copy)
    for copy in copies:
        copy.wait()


def pack(info, slots, arrays, deps):
    heads = len(slots)
    return pl.pallas_call(
        spread(functools.partial(pack_kernel, heads, slots), 5, deps),
        out_shape=[jax.ShapeDtypeStruct((heads, 4, ROWS, HEAD_DIM), jnp.bfloat16)] * 4,
        in_specs=[pl.BlockSpec(memory_space=pltpu.SMEM)] + [hbm_spec] * 4 + [any_spec] * len(deps),
        out_specs=[any_spec] * 4,
        scratch_shapes=[pltpu.SemaphoreType.DMA((heads * 16,))],
        compiler_params=pltpu.CompilerParams(vmem_limit_bytes=4 * 2**20),
        cost_estimate=pl.CostEstimate(flops=0, bytes_accessed=heads * 1600000, transcendentals=0),
        name="pack",
    )(info, *arrays, *deps)


def order_kernel(heads, info, r0, r1, r2, r3, out, sem):
    copies = []
    for k, src in enumerate((r0, r1, r2, r3)):
        row = pl.multiple_of(info[4 + k] * ROWS, ROWS)
        for h in range(heads):
            for a in range(2):
                copy = pltpu.make_async_copy(
                    src.at[h, a], out.at[h, a, pl.ds(row, ROWS)], sem.at[len(copies)]
                )
                copy.start()
                copies.append(copy)
    for copy in copies:
        copy.wait()


def order_halo(info, received, deps):
    heads = received[0].shape[0]
    return pl.pallas_call(
        spread(functools.partial(order_kernel, heads), 5, deps),
        out_shape=jax.ShapeDtypeStruct((heads, 2, SPAN, HEAD_DIM), jnp.bfloat16),
        in_specs=[pl.BlockSpec(memory_space=pltpu.SMEM)] + [any_spec] * (4 + len(deps)),
        out_specs=any_spec,
        scratch_shapes=[pltpu.SemaphoreType.DMA((heads * 8,))],
        compiler_params=pltpu.CompilerParams(vmem_limit_bytes=4 * 2**20),
        cost_estimate=pl.CostEstimate(flops=0, bytes_accessed=heads * 800000, transcendentals=0),
        name="order",
    )(info, *received, *deps)


def dot_nt(a, b):
    return lax.dot_general(a, b, (((1,), (1,)), ((), ())), preferred_element_type=jnp.float32)


def dot_tn(a, b):
    return lax.dot_general(a, b, (((0,), (0,)), ((), ())), preferred_element_type=jnp.float32)


def main_kernel(
    info, lams, gain_ref, starts_ref, r0, r1, r2, r3, prev_ref,
    dq_ref, own_ref, back_ref, q_s, g_s, k_w, v_w, dk_s, dv_s,
):
    head = pl.program_id(0)
    k_w[:SPAN] = prev_ref[0, 0]
    v_w[:SPAN] = prev_ref[0, 1]
    for k, src in enumerate((r0, r1, r2, r3)):
        row = pl.multiple_of(info[4 + k] * ROWS, ROWS)
        k_w[pl.ds(SPAN + row, ROWS)] = src[0, 0]
        v_w[pl.ds(SPAN + row, ROWS)] = src[0, 1]
        q_s[pl.ds(row, ROWS)] = src[0, 2]
        g_s[pl.ds(row, ROWS)] = src[0, 3]
    dk_s[...] = jnp.zeros_like(dk_s)
    dv_s[...] = jnp.zeros_like(dv_s)
    lam = lams[head]

    def tile(i, n):
        width = n * TILE
        row = pl.multiple_of(i * TILE, TILE)
        left = pl.multiple_of((4 + i - n) * TILE, TILE)
        rows, cols = pl.ds(row, TILE), pl.ds(left, width)
        k, v = k_w[cols], v_w[cols]
        first = lax.broadcasted_iota(jnp.int32, (TILE, HEAD_DIM), 1) < HEAD_DIM // 2
        q = (q_s[rows].astype(jnp.float32) * score_scale)
        q_two = jnp.concatenate(
            [jnp.where(first, q, 0.0), jnp.where(first, 0.0, q)], axis=0
        ).astype(jnp.bfloat16)
        scores = dot_nt(q_two, k)
        spot = lax.broadcasted_iota(jnp.int32, (TILE, width), 1) + left
        own = lax.broadcasted_iota(jnp.int32, (TILE, width), 0) + (row + SPAN)
        live = (spot >= starts_ref[rows]) & (spot <= own)

        def soft(score):
            score = jnp.where(live, score, masked_value)
            raised = jnp.exp(score - jnp.max(score, axis=1, keepdims=True))
            return raised * (1.0 / jnp.sum(raised, axis=1, keepdims=True))

        prob_one, prob_two = soft(scores[:TILE]), soft(scores[TILE:])
        prob_one_b, prob_two_b = prob_one.astype(jnp.bfloat16), prob_two.astype(jnp.bfloat16)
        out_one = jnp.dot(prob_one_b, v, preferred_element_type=jnp.float32)
        out_two = jnp.dot(prob_two_b, v, preferred_element_type=jnp.float32)
        attended = out_one - lam * out_two
        scaled = g_s[rows].astype(jnp.float32) * gain_ref[...] * (1.0 - lambda_init)
        inv_rms = lax.rsqrt(jnp.mean(attended * attended, axis=1, keepdims=True) + norm_epsilon)
        d_att = inv_rms * scaled - attended * (inv_rms * inv_rms * inv_rms) * jnp.mean(
            attended * scaled, axis=1, keepdims=True
        )
        d_att_b = d_att.astype(jnp.bfloat16)
        delta_one = jnp.sum(d_att * out_one, axis=1, keepdims=True)
        delta_two = -lam * jnp.sum(d_att * out_two, axis=1, keepdims=True)
        grad_probs = dot_nt(d_att_b, v)
        ds_one = (prob_one * (grad_probs - delta_one)).astype(jnp.bfloat16)
        ds_two = (prob_two * (-lam * grad_probs - delta_two)).astype(jnp.bfloat16)
        dq_one = jnp.dot(ds_one, k, preferred_element_type=jnp.float32)
        dq_two = jnp.dot(ds_two, k, preferred_element_type=jnp.float32)
        dq_ref[0, rows] = (jnp.where(first, dq_one, dq_two) * score_scale).astype(jnp.bfloat16)
        dk_s[cols] += dot_tn(ds_one, q_two[:TILE]) + dot_tn(ds_two, q_two[TILE:])
        dv_s[cols] += dot_tn(prob_one_b, d_att_b) - lam * dot_tn(prob_two_b, d_att_b)

    def step(i, carry):
        tiles = info[10 + i]
        for n in range(1, 5):
            pl.when(tiles == n)(functools.partial(tile, i, n))
        return carry

    lax.fori_loop(0, SPAN // TILE, step, 0)
    back_ref[0, 0] = dk_s[:SPAN].astype(jnp.bfloat16)
    back_ref[0, 1] = dv_s[:SPAN].astype(jnp.bfloat16)
    own_ref[0, 0] = dk_s[SPAN:]
    own_ref[0, 1] = dv_s[SPAN:]


def attend(info, lams, gain, starts, received, prev, deps):
    heads = prev.shape[0]
    smem = pl.BlockSpec(memory_space=pltpu.SMEM)
    return pl.pallas_call(
        spread(main_kernel, 9, deps),
        grid=(heads,),
        out_shape=[
            jax.ShapeDtypeStruct((heads, SPAN, HEAD_DIM), jnp.bfloat16),
            jax.ShapeDtypeStruct((heads, 2, SPAN, HEAD_DIM), jnp.float32),
            jax.ShapeDtypeStruct((heads, 2, SPAN, HEAD_DIM), jnp.bfloat16),
        ],
        in_specs=[
            smem,
            smem,
            pl.BlockSpec((1, HEAD_DIM), lambda h: (0, 0)),
            pl.BlockSpec((SPAN, 1), lambda h: (0, 0)),
        ]
        + [pl.BlockSpec((1, 4, ROWS, HEAD_DIM), lambda h: (h, 0, 0, 0))] * 4
        + [pl.BlockSpec((1, 2, SPAN, HEAD_DIM), lambda h: (h, 0, 0, 0))]
        + [any_spec] * len(deps),
        out_specs=[
            pl.BlockSpec((1, SPAN, HEAD_DIM), lambda h: (h, 0, 0)),
            pl.BlockSpec((1, 2, SPAN, HEAD_DIM), lambda h: (h, 0, 0, 0)),
            pl.BlockSpec((1, 2, SPAN, HEAD_DIM), lambda h: (h, 0, 0, 0)),
        ],
        scratch_shapes=[
            pltpu.VMEM((SPAN, HEAD_DIM), jnp.bfloat16),
            pltpu.VMEM((SPAN, HEAD_DIM), jnp.bfloat16),
            pltpu.VMEM((2 * SPAN, HEAD_DIM), jnp.bfloat16),
            pltpu.VMEM((2 * SPAN, HEAD_DIM), jnp.bfloat16),
            pltpu.VMEM((2 * SPAN, HEAD_DIM), jnp.float32),
            pltpu.VMEM((2 * SPAN, HEAD_DIM), jnp.float32),
        ],
        compiler_params=pltpu.CompilerParams(vmem_limit_bytes=32 * 2**20),
        cost_estimate=pl.CostEstimate(
            flops=heads * 6 * 10**9, bytes_accessed=heads * 3 * 10**6, transcendentals=heads * 10**6
        ),
        name="attend",
    )(info, lams, gain, starts, *received, prev, *deps)


def merge_kernel(info, dq_ref, own_ref, halo_ref, *outs):
    for k, out in enumerate(outs):
        rows = pl.ds(pl.multiple_of(info[4 + k] * ROWS, ROWS), ROWS)
        out[0, 0] = dq_ref[0, rows]
        for a in range(2):
            out[0, 1 + a] = (own_ref[0, a, rows] + halo_ref[0, a, rows].astype(jnp.float32)).astype(
                jnp.bfloat16
            )


def merge(info, dq, own, halo, deps):
    heads = dq.shape[0]
    return pl.pallas_call(
        spread(merge_kernel, 4, deps),
        grid=(heads,),
        out_shape=[jax.ShapeDtypeStruct((heads, 3, ROWS, HEAD_DIM), jnp.bfloat16)] * 4,
        in_specs=[
            pl.BlockSpec(memory_space=pltpu.SMEM),
            pl.BlockSpec((1, SPAN, HEAD_DIM), lambda h: (h, 0, 0)),
            pl.BlockSpec((1, 2, SPAN, HEAD_DIM), lambda h: (h, 0, 0, 0)),
            pl.BlockSpec((1, 2, SPAN, HEAD_DIM), lambda h: (h, 0, 0, 0)),
        ]
        + [any_spec] * len(deps),
        out_specs=[pl.BlockSpec((1, 3, ROWS, HEAD_DIM), lambda h: (h, 0, 0, 0))] * 4,
        compiler_params=pltpu.CompilerParams(vmem_limit_bytes=8 * 2**20),
        cost_estimate=pl.CostEstimate(flops=0, bytes_accessed=heads * 2000000, transcendentals=0),
        name="merge",
    )(info, dq, own, halo, *deps)


def unpack_kernel(heads_of, groups, *refs):
    count = sum(4 for _ in heads_of)
    srcs, outs, sem = refs[:count], refs[count:count + 3], refs[count + 3]
    copies = []
    for s, slots in enumerate(heads_of):
        for k in range(4):
            for h, slot in enumerate(slots):
                col = pl.multiple_of((slot * GROUPS + groups[s, k]) * HEAD_DIM, HEAD_DIM)
                for a in range(3):
                    copy = pltpu.make_async_copy(
                        srcs[s * 4 + k].at[h, a], outs[a].at[:, pl.ds(col, HEAD_DIM)],
                        sem.at[len(copies)],
                    )
                    copy.start()
                    copies.append(copy)
    for copy in copies:
        copy.wait()


def unpack(groups, heads_of, buffers, width):
    return pl.pallas_call(
        functools.partial(unpack_kernel, heads_of),
        out_shape=[jax.ShapeDtypeStruct((ROWS, width), jnp.bfloat16)] * 3,
        in_specs=[pl.BlockSpec(memory_space=pltpu.SMEM)] + [any_spec] * len(buffers),
        out_specs=[any_spec] * 3,
        scratch_shapes=[pltpu.SemaphoreType.DMA((sum(map(len, heads_of)) * 12,))],
        compiler_params=pltpu.CompilerParams(vmem_limit_bytes=4 * 2**20),
        name="unpack",
    )(groups, *buffers)


def per_device(queries, keys, values, grad_out, lambdas, norm_gain, doc_lengths):
    axes = ("cp", "hp")
    me = lax.axis_index("cp") * lax.axis_size("hp") + lax.axis_index("hp")
    plans = [Plan(0), Plan(1)]
    doc_ends = jnp.cumsum(doc_lengths)
    tables, starts_of = [], []
    for plan in plans:
        line = jnp.asarray(plan.table)[me]
        at = line[8] * SPAN + jnp.arange(SPAN, dtype=jnp.int32)
        begin = jnp.max(
            jnp.where(doc_ends[None, :] <= at[:, None], doc_ends[None, :], 0), axis=1
        ) - (line[8] - 1) * SPAN
        tiles = 4 + jnp.arange(3, dtype=jnp.int32) - begin[::TILE] // TILE
        tables.append(jnp.concatenate([line, tiles]))
        starts_of.append(begin[:, None])
    gain = norm_gain[None, :]
    arrays = (keys, values, queries, grad_out)
    state = [{} for _ in STAGES]
    for step in ORDER:
        step, *waits = step.split("<")
        index = int(step[1:])
        plan, info, now = plans[index % 2], tables[index % 2], state[index]
        slots = STAGES[index]
        deps = tuple(state[int(wait[1:])][wait[0]] for wait in waits)
        deps = tuple(b for dep in deps for b in (dep if isinstance(dep, list) else [dep]))
        if step[0] == "P":
            made = pack(info, slots, arrays, deps)
            now["P"] = made[0]
            now["R"] = [lax.ppermute(b, axes, r) for b, r in zip(made, plan.out_routes)]
        elif step[0] == "O":
            now["O"] = order_halo(info, now["R"], deps)
            now["H"] = lax.ppermute(now["O"], axes, plan.halo_route)
        elif step[0] == "A":
            lams = jnp.stack([lambdas[slot * GROUPS + info[9]] for slot in slots])
            now["A"], now["own"], back = attend(
                info, lams, gain, starts_of[index % 2], now["R"], now["H"], deps
            )
            now["B"] = lax.ppermute(back, axes, plan.halo_back)
        else:
            made = merge(info, now["A"], now["own"], now["B"], deps)
            now["M"] = made[0]
            now["X"] = [lax.ppermute(b, axes, r) for b, r in zip(made, plan.back_routes)]
    finals = [b for now in state for b in now["X"]]
    groups = jnp.stack([tables[index % 2][:4] for index in range(len(STAGES))])
    return tuple(unpack(groups, STAGES, finals, queries.shape[1]))


def solution(mesh):
    spec = P(("cp", "hp"), None)
    return jax.shard_map(
        per_device,
        mesh=mesh,
        in_specs=(spec,) * 4 + (P(),) * 3,
        out_specs=(spec,) * 3,
        check_vma=False,
    )
```

```python
import functools

import jax
import jax.numpy as jnp
from jax import lax
from jax.experimental import pallas as pl
from jax.experimental.pallas import tpu as pltpu
from jax.sharding import Mesh, PartitionSpec as P

HEAD_DIM = 128
SPAN = 768
ROWS = 192
TILE = 256
COLUMN = 16
LATE = 4
score_scale = 0.125
norm_epsilon = 1e-05
lambda_init = 0.8
masked_value = -1e30
AXES = ("col", "quad", "hp")

any_spec = pl.BlockSpec(memory_space=pl.ANY)
smem_spec = pl.BlockSpec(memory_space=pltpu.SMEM)
vmem_spec = pl.BlockSpec(memory_space=pltpu.VMEM)


def spread(kernel, inputs, deps):
    def ordered(*refs):
        kernel(*refs[:inputs], *refs[inputs + len(deps):])

    return ordered


def run_copies(pairs, sem):
    copies = [pltpu.make_async_copy(a, b, sem.at[i]) for i, (a, b) in enumerate(pairs)]
    for copy in copies:
        copy.start()
    for copy in copies:
        copy.wait()


def columns(head):
    start = head * HEAD_DIM
    return pl.ds(start if isinstance(head, int) else pl.multiple_of(start, HEAD_DIM), HEAD_DIM)


def pack_kernel(k_ref, v_ref, q_ref, g_ref, out, sem):
    run_copies(
        [
            (src.at[:, columns(h)], out.at[h, a])
            for h in range(COLUMN)
            for a, src in enumerate((k_ref, v_ref, q_ref, g_ref))
        ],
        sem,
    )


def pack_column(arrays):
    return pl.pallas_call(
        pack_kernel,
        out_shape=jax.ShapeDtypeStruct((COLUMN, 4, ROWS, HEAD_DIM), jnp.bfloat16),
        in_specs=[any_spec] * 4,
        out_specs=any_spec,
        scratch_shapes=[pltpu.SemaphoreType.DMA((COLUMN * 4,))],
        compiler_params=pltpu.CompilerParams(vmem_limit_bytes=4 * 2**20),
        cost_estimate=pl.CostEstimate(flops=0, bytes_accessed=6 * 10**6, transcendentals=0),
        name="pack_column",
    )(*arrays)


def pack_late_kernel(hp_ref, k_ref, v_ref, q_ref, g_ref, *rest):
    outs, sem = rest[:4], rest[4]
    run_copies(
        [
            (src.at[:, columns(COLUMN + lax.rem(hp_ref[0] + k, 4))], outs[k].at[a])
            for k in range(4)
            for a, src in enumerate((k_ref, v_ref, q_ref, g_ref))
        ],
        sem,
    )


def pack_late(hp, arrays, deps):
    return pl.pallas_call(
        spread(pack_late_kernel, 5, deps),
        out_shape=[jax.ShapeDtypeStruct((4, ROWS, HEAD_DIM), jnp.bfloat16)] * 4,
        in_specs=[smem_spec] + [any_spec] * (4 + len(deps)),
        out_specs=[any_spec] * 4,
        scratch_shapes=[pltpu.SemaphoreType.DMA((16,))],
        compiler_params=pltpu.CompilerParams(vmem_limit_bytes=4 * 2**20),
        cost_estimate=pl.CostEstimate(flops=0, bytes_accessed=16 * 10**5, transcendentals=0),
        name="pack_late",
    )(hp, *arrays, *deps)


def halo_kernel(l0, l1, l2, l3, out, sem):
    run_copies([(src.at[pl.ds(0, 2)], out.at[k]) for k, src in enumerate((l0, l1, l2, l3))], sem)


def late_halo_rows(blocks, deps):
    return pl.pallas_call(
        spread(halo_kernel, 4, deps),
        out_shape=jax.ShapeDtypeStruct((4, 2, ROWS, HEAD_DIM), jnp.bfloat16),
        in_specs=[any_spec] * (4 + len(deps)),
        out_specs=any_spec,
        scratch_shapes=[pltpu.SemaphoreType.DMA((4,))],
        compiler_params=pltpu.CompilerParams(vmem_limit_bytes=4 * 2**20),
        cost_estimate=pl.CostEstimate(flops=0, bytes_accessed=8 * 10**5, transcendentals=0),
        name="late_halo_rows",
    )(*blocks, *deps)


def dot_nt(a, b):
    return lax.dot_general(a, b, (((1,), (1,)), ((), ())), preferred_element_type=jnp.float32)


def dot_tn(a, b):
    return lax.dot_general(a, b, (((0,), (0,)), ((), ())), preferred_element_type=jnp.float32)


def attend_kernel(
    first_tile, last_tile, blocks, has_prev, late, scal, lam_ref, gain_ref, ends_ref, *refs
):
    recv = refs[:4] if late else refs[:1]
    refs = refs[len(recv):]
    prev_ref = refs[0] if has_prev else None
    refs = refs[1:] if has_prev else refs
    dq_ref, dkv_ref = refs[:2]
    back_ref = refs[2] if has_prev else None
    q_s, g_s, k_w, v_w, dk_s, dv_s = refs[-6:]
    lam = lam_ref[0]

    def place(index):
        if not late:
            return index * ROWS
        return pl.multiple_of(lax.rem(scal[0] + 4 - index, 4) * ROWS, ROWS)

    shift = first_tile * TILE
    for index in range(blocks):
        block = recv[index] if late else recv[0].at[index]
        if late or (index + 1) * ROWS > shift - SPAN and index * ROWS < last_tile * TILE:
            row = place(index)
            low = 0 if late else max(0, shift - SPAN - index * ROWS)
            high = ROWS if late else min(ROWS, last_tile * TILE - index * ROWS)
            k_w[pl.ds(SPAN + row + low - shift, high - low)] = block[0, low:high]
            v_w[pl.ds(SPAN + row + low - shift, high - low)] = block[1, low:high]
        if late or (index + 1) * ROWS > shift and index * ROWS < last_tile * TILE:
            row = place(index)
            low = 0 if late else max(0, shift - index * ROWS)
            high = ROWS if late else min(ROWS, last_tile * TILE - index * ROWS)
            q_s[pl.ds(row + low - shift, high - low)] = block[2, low:high]
            g_s[pl.ds(row + low - shift, high - low)] = block[3, low:high]
    if has_prev:
        for index in range(4):
            row = place(index)
            k_w[pl.ds(row, ROWS)] = prev_ref[index, 0]
            v_w[pl.ds(row, ROWS)] = prev_ref[index, 1]
    dk_s[...] = jnp.zeros_like(dk_s)
    dv_s[...] = jnp.zeros_like(dv_s)

    def tile(i, n):
        width = n * TILE
        row = pl.multiple_of(i * TILE, TILE)
        left = pl.multiple_of((4 + i - n) * TILE, TILE)
        rows, cols = pl.ds(row, TILE), pl.ds(left, width)
        k, v = k_w[cols], v_w[cols]
        first = lax.broadcasted_iota(jnp.int32, (TILE, HEAD_DIM), 1) < HEAD_DIM // 2
        q = q_s[rows].astype(jnp.float32) * score_scale
        q_two = jnp.concatenate(
            [jnp.where(first, q, 0.0), jnp.where(first, 0.0, q)], axis=0
        ).astype(jnp.bfloat16)
        scores = dot_nt(q_two, k)
        base = scal[1] + shift
        spot = lax.broadcasted_iota(jnp.int32, (TILE, width), 1) + (base - SPAN + left)
        own = lax.broadcasted_iota(jnp.int32, (TILE, width), 0) + (base + row)
        at = lax.broadcasted_iota(jnp.int32, (TILE, HEAD_DIM), 0) + (base + row)
        ends = ends_ref[...]
        begin = jnp.max(jnp.where(ends <= at, ends, 0), axis=1, keepdims=True)
        live = (spot >= begin) & (spot <= own)

        def soft(score):
            score = jnp.where(live, score, masked_value)
            raised = jnp.exp(score - jnp.max(score, axis=1, keepdims=True))
            return raised * (1.0 / jnp.sum(raised, axis=1, keepdims=True))

        prob_one, prob_two = soft(scores[:TILE]), soft(scores[TILE:])
        prob_one_b, prob_two_b = prob_one.astype(jnp.bfloat16), prob_two.astype(jnp.bfloat16)
        out_one = jnp.dot(prob_one_b, v, preferred_element_type=jnp.float32)
        out_two = jnp.dot(prob_two_b, v, preferred_element_type=jnp.float32)
        attended = out_one - lam * out_two
        scaled = g_s[rows].astype(jnp.float32) * gain_ref[...] * (1.0 - lambda_init)
        inv_rms = lax.rsqrt(jnp.mean(attended * attended, axis=1, keepdims=True) + norm_epsilon)
        d_att = inv_rms * scaled - attended * (inv_rms * inv_rms * inv_rms) * jnp.mean(
            attended * scaled, axis=1, keepdims=True
        )
        d_att_b = d_att.astype(jnp.bfloat16)
        delta_one = jnp.sum(d_att * out_one, axis=1, keepdims=True)
        delta_two = -lam * jnp.sum(d_att * out_two, axis=1, keepdims=True)
        grad_probs = dot_nt(d_att_b, v)
        ds_one = (prob_one * (grad_probs - delta_one)).astype(jnp.bfloat16)
        ds_two = (prob_two * (-lam * grad_probs - delta_two)).astype(jnp.bfloat16)
        dq_one = jnp.dot(ds_one, k, preferred_element_type=jnp.float32)
        dq_two = jnp.dot(ds_two, k, preferred_element_type=jnp.float32)
        dq_ref[rows] = (jnp.where(first, dq_one, dq_two) * score_scale).astype(jnp.bfloat16)
        dk_s[cols] += dot_tn(ds_one, q_two[:TILE]) + dot_tn(ds_two, q_two[TILE:])
        dv_s[cols] += dot_tn(prob_one_b, d_att_b) - lam * dot_tn(prob_two_b, d_att_b)

    def step(i, carry):
        tiles = scal[2 + first_tile + i]
        for n in range(1, 5):
            pl.when(tiles == n)(functools.partial(tile, i, n))
        return carry

    lax.fori_loop(0, last_tile - first_tile, step, 0)
    if has_prev:
        back_ref[0] = dk_s[:SPAN].astype(jnp.bfloat16)
        back_ref[1] = dv_s[:SPAN].astype(jnp.bfloat16)
        dkv_ref[0] = dk_s[SPAN:]
        dkv_ref[1] = dv_s[SPAN:]
    else:
        dkv_ref[0] = dk_s[...]
        dkv_ref[1] = dv_s[...]


def attend(name, tiles, scal, lam, gain, ends, recv, prev, deps=()):
    late = isinstance(recv, list)
    blocks = len(recv) if late else recv.shape[0]
    recv = recv if late else [recv]
    first_tile, last_tile = tiles
    queries = (last_tile - first_tile) * TILE
    window = queries + SPAN
    has_prev = prev is not None
    out_shape = [
        jax.ShapeDtypeStruct((queries, HEAD_DIM), jnp.bfloat16),
        jax.ShapeDtypeStruct((2, queries if has_prev else window, HEAD_DIM), jnp.float32),
    ]
    if has_prev:
        out_shape.append(jax.ShapeDtypeStruct((2, SPAN, HEAD_DIM), jnp.bfloat16))
    inputs = [scal, lam, gain, ends, *recv] + ([prev] if has_prev else [])
    body = functools.partial(attend_kernel, first_tile, last_tile, blocks, has_prev, late)
    count = last_tile - first_tile
    return pl.pallas_call(
        spread(body, len(inputs), deps),
        out_shape=out_shape,
        in_specs=[smem_spec] * 2 + [vmem_spec] * (len(inputs) - 2) + [any_spec] * len(deps),
        out_specs=[vmem_spec] * len(out_shape),
        scratch_shapes=[
            pltpu.VMEM((queries, HEAD_DIM), jnp.bfloat16),
            pltpu.VMEM((queries, HEAD_DIM), jnp.bfloat16),
            pltpu.VMEM((window, HEAD_DIM), jnp.bfloat16),
            pltpu.VMEM((window, HEAD_DIM), jnp.bfloat16),
            pltpu.VMEM((window, HEAD_DIM), jnp.float32),
            pltpu.VMEM((window, HEAD_DIM), jnp.float32),
        ],
        compiler_params=pltpu.CompilerParams(vmem_limit_bytes=36 * 2**20),
        cost_estimate=pl.CostEstimate(
            flops=count * 2 * 10**9, bytes_accessed=count * 10**6, transcendentals=count * 3 * 10**5
        ),
        name=name,
    )(*inputs, *deps)


def merge_column_kernel(dq_b, dkv_b, dq_a, dkv_a, dq_c, dkv_c, dq_d, dkv_d, halo_ref, out, dq_s, sum_s):
    dq_s[0:768] = dq_a[...]
    dq_s[768:1792] = dq_b[...]
    dq_s[1792:2304] = dq_c[...]
    dq_s[2304:3072] = dq_d[...]
    for a in range(2):
        sum_s[a, 0:768] = dkv_b[a, 0:768] + dkv_a[a]
        sum_s[a, 768:1024] = dkv_b[a, 768:1024]
        sum_s[a, 1024:1536] = dkv_b[a, 1024:1536] + dkv_c[a, 0:512]
        sum_s[a, 1536:1792] = dkv_b[a, 1536:1792] + dkv_c[a, 512:768] + dkv_d[a, 0:256]
        sum_s[a, 1792:2304] = dkv_c[a, 768:1280] + dkv_d[a, 256:768]
        sum_s[a, 2304:3072] = dkv_d[a, 768:1536] + halo_ref[a].astype(jnp.float32)
    for b in range(COLUMN):
        rows = slice(b * ROWS, (b + 1) * ROWS)
        out[b, 0] = dq_s[rows]
        out[b, 1] = sum_s[0, rows].astype(jnp.bfloat16)
        out[b, 2] = sum_s[1, rows].astype(jnp.bfloat16)


def merge_column(parts, halo, deps=()):
    run = COLUMN * ROWS
    return pl.pallas_call(
        spread(merge_column_kernel, 9, deps),
        out_shape=jax.ShapeDtypeStruct((COLUMN, 3, ROWS, HEAD_DIM), jnp.bfloat16),
        in_specs=[vmem_spec] * 9 + [any_spec] * len(deps),
        out_specs=vmem_spec,
        scratch_shapes=[
            pltpu.VMEM((run, HEAD_DIM), jnp.bfloat16),
            pltpu.VMEM((2, run, HEAD_DIM), jnp.float32),
        ],
        compiler_params=pltpu.CompilerParams(vmem_limit_bytes=24 * 2**20),
        cost_estimate=pl.CostEstimate(flops=0, bytes_accessed=8 * 10**6, transcendentals=0),
        name="merge_column",
    )(*parts, halo, *deps)


def merge_late_kernel(hp_ref, dq_ref, dkv_ref, halo_ref, *outs):
    for k, out in enumerate(outs):
        rows = pl.ds(pl.multiple_of(lax.rem(hp_ref[0] + 4 - k, 4) * ROWS, ROWS), ROWS)
        out[0] = dq_ref[rows]
        for a in range(2):
            out[1 + a] = (dkv_ref[a, rows] + halo_ref[a, rows].astype(jnp.float32)).astype(
                jnp.bfloat16
            )


def merge_late(hp, dq, dkv, halo, deps=()):
    return pl.pallas_call(
        spread(merge_late_kernel, 4, deps),
        out_shape=[jax.ShapeDtypeStruct((3, ROWS, HEAD_DIM), jnp.bfloat16)] * 4,
        in_specs=[smem_spec] + [vmem_spec] * 3 + [any_spec] * len(deps),
        out_specs=[vmem_spec] * 4,
        compiler_params=pltpu.CompilerParams(vmem_limit_bytes=8 * 2**20),
        cost_estimate=pl.CostEstimate(flops=0, bytes_accessed=2 * 10**6, transcendentals=0),
        name="merge_late",
    )(hp, dq, dkv, halo, *deps)


def unpack_kernel(hp_ref, col_ref, l0, l1, l2, l3, *rest):
    outs, sem = rest[:3], rest[3]
    pairs = [
        (col_ref.at[h, a], outs[a].at[:, columns(h)]) for a in range(3) for h in range(COLUMN)
    ]
    for k, src in enumerate((l0, l1, l2, l3)):
        cols = columns(COLUMN + lax.rem(hp_ref[0] + k, 4))
        pairs += [(src.at[a], outs[a].at[:, cols]) for a in range(3)]
    run_copies(pairs, sem)


def unpack(hp, column, late, width):
    return pl.pallas_call(
        unpack_kernel,
        out_shape=[jax.ShapeDtypeStruct((ROWS, width), jnp.bfloat16)] * 3,
        in_specs=[smem_spec] + [any_spec] * 5,
        out_specs=[any_spec] * 3,
        scratch_shapes=[pltpu.SemaphoreType.DMA((60,))],
        compiler_params=pltpu.CompilerParams(vmem_limit_bytes=4 * 2**20),
        name="unpack",
    )(hp, column, *late)


def per_device(queries, keys, values, grad_out, lambdas, norm_gain, doc_lengths):
    col, quad, hp = (lax.axis_index(a) for a in AXES)
    hp_s = hp[None].astype(jnp.int32)
    doc_ends = jnp.cumsum(doc_lengths)
    ends = doc_ends[None, :]
    gain = norm_gain[None, :]

    def scalars(start, tiles):
        at = start + TILE * jnp.arange(tiles, dtype=jnp.int32)
        begin = jnp.max(jnp.where(ends <= at[:, None], ends, 0), axis=1)
        count = 4 + jnp.arange(tiles, dtype=jnp.int32) - (begin - (start - SPAN)) // TILE
        return jnp.concatenate([hp_s, start[None], count]).astype(jnp.int32)

    column_scal = scalars(col * (COLUMN * ROWS), 12)
    late_scal = scalars((col * 4 + quad) * SPAN, 3)
    column_lam = lax.dynamic_slice_in_dim(lambdas, quad * 4 + hp, 1)
    late_lam = lax.dynamic_slice_in_dim(lambdas, COLUMN + hp, 1)
    arrays = (keys, values, queries, grad_out)

    chunk = [(d, d + 4) for d in range(252)]
    run = [(d, d + 16) for d in range(240)]
    turn = [[(d, d // 4 * 4 + (d + k) % 4) for d in range(256)] for k in range(4)]

    def back(route):
        return [(b, a) for a, b in route]

    def send(block, route):
        return lax.ppermute(block, AXES, route)

    packed = pack_column(arrays)
    recv = lax.all_to_all(packed, ("quad", "hp"), split_axis=0, concat_axis=0, tiled=True)
    late_sent = pack_late(hp_s, arrays, (packed,))
    late_recv = [late_sent[0]] + [send(late_sent[k], turn[k]) for k in range(1, 4)]
    prev = send(recv[12:, :2], run)

    b_part = attend("attend_b", (3, 7), column_scal, column_lam, gain, ends, recv, None, (late_sent[0],))
    late_prev = send(late_halo_rows(late_recv, (b_part[0],)), chunk)
    a_part = attend("attend_a", (0, 3), column_scal, column_lam, gain, ends, recv, prev, (b_part[0],))
    halo = send(a_part[2], back(run))
    late_part = attend(
        "attend_late", (0, 3), late_scal, late_lam, gain, ends, late_recv, late_prev, (a_part[0],)
    )
    late_halo = send(late_part[2], back(chunk))
    c_part = attend("attend_c", (7, 9), column_scal, column_lam, gain, ends, recv, None, (late_part[0],))
    late_merged = merge_late(hp_s, late_part[0], late_part[1], late_halo, (c_part[0],))
    late = [late_merged[0]] + [send(late_merged[k], back(turn[k])) for k in range(1, 4)]
    d_part = attend("attend_d", (9, 12), column_scal, column_lam, gain, ends, recv, None, (late_merged[0],))
    merged = merge_column((*b_part, *a_part[:2], *c_part, *d_part), halo, tuple(late[1:]))
    column = lax.all_to_all(merged, ("quad", "hp"), split_axis=0, concat_axis=0, tiled=True)
    return tuple(unpack(hp_s, column, late, queries.shape[1]))


def solution(mesh):
    grid = Mesh(mesh.devices.reshape(16, 4, 4), AXES)
    spec = P(AXES, None)
    return jax.shard_map(
        per_device,
        mesh=grid,
        in_specs=(spec,) * 4 + (P(),) * 3,
        out_specs=(spec,) * 3,
        check_vma=False,
    )
```

```python
import functools

import jax
import jax.numpy as jnp
from jax import lax
from jax.experimental import pallas as pl
from jax.experimental.pallas import tpu as pltpu
from jax.sharding import Mesh, PartitionSpec as P

HEAD_DIM = 128
SPAN = 768
ROWS = 192
TILE = 256
COLUMN = 16
LATE = 4
score_scale = 0.125
norm_epsilon = 1e-05
lambda_init = 0.8
masked_value = -1e30
AXES = ("col", "z_lo", "core", "hp")
RING = ("core", "z_lo", "hp")

PLACE = [(b // 4 % 2 * 2 + b // 8) * 4 + b % 4 for b in range(COLUMN)]

any_spec = pl.BlockSpec(memory_space=pl.ANY)
smem_spec = pl.BlockSpec(memory_space=pltpu.SMEM)
vmem_spec = pl.BlockSpec(memory_space=pltpu.VMEM)


def spread(kernel, inputs, deps):
    def ordered(*refs):
        kernel(*refs[:inputs], *refs[inputs + len(deps):])

    return ordered


def run_copies(pairs, sem):
    copies = [pltpu.make_async_copy(a, b, sem.at[i]) for i, (a, b) in enumerate(pairs)]
    for copy in copies:
        copy.start()
    for copy in copies:
        copy.wait()


def columns(head):
    start = head * HEAD_DIM
    return pl.ds(start if isinstance(head, int) else pl.multiple_of(start, HEAD_DIM), HEAD_DIM)


def pack_kernel(k_ref, v_ref, q_ref, g_ref, out, sem):
    run_copies(
        [
            (src.at[:, columns(h)], out.at[h, a])
            for h in range(COLUMN)
            for a, src in enumerate((k_ref, v_ref, q_ref, g_ref))
        ],
        sem,
    )


def pack_column(arrays):
    return pl.pallas_call(
        pack_kernel,
        out_shape=jax.ShapeDtypeStruct((COLUMN, 4, ROWS, HEAD_DIM), jnp.bfloat16),
        in_specs=[any_spec] * 4,
        out_specs=any_spec,
        scratch_shapes=[pltpu.SemaphoreType.DMA((COLUMN * 4,))],
        compiler_params=pltpu.CompilerParams(vmem_limit_bytes=4 * 2**20),
        cost_estimate=pl.CostEstimate(flops=0, bytes_accessed=6 * 10**6, transcendentals=0),
        name="pack_column",
    )(*arrays)


def pack_late_kernel(hp_ref, k_ref, v_ref, q_ref, g_ref, *rest):
    outs, sem = rest[:4], rest[4]
    run_copies(
        [
            (src.at[:, columns(COLUMN + lax.rem(hp_ref[0] + k, 4))], outs[k].at[a])
            for k in range(4)
            for a, src in enumerate((k_ref, v_ref, q_ref, g_ref))
        ],
        sem,
    )


def pack_late(hp, arrays, deps):
    return pl.pallas_call(
        spread(pack_late_kernel, 5, deps),
        out_shape=[jax.ShapeDtypeStruct((4, ROWS, HEAD_DIM), jnp.bfloat16)] * 4,
        in_specs=[smem_spec] + [any_spec] * (4 + len(deps)),
        out_specs=[any_spec] * 4,
        scratch_shapes=[pltpu.SemaphoreType.DMA((16,))],
        compiler_params=pltpu.CompilerParams(vmem_limit_bytes=4 * 2**20),
        cost_estimate=pl.CostEstimate(flops=0, bytes_accessed=16 * 10**5, transcendentals=0),
        name="pack_late",
    )(hp, *arrays, *deps)


def halo_kernel(l0, l1, l2, l3, out, sem):
    run_copies([(src.at[pl.ds(0, 2)], out.at[k]) for k, src in enumerate((l0, l1, l2, l3))], sem)


def late_halo_rows(blocks, deps):
    return pl.pallas_call(
        spread(halo_kernel, 4, deps),
        out_shape=jax.ShapeDtypeStruct((4, 2, ROWS, HEAD_DIM), jnp.bfloat16),
        in_specs=[any_spec] * (4 + len(deps)),
        out_specs=any_spec,
        scratch_shapes=[pltpu.SemaphoreType.DMA((4,))],
        compiler_params=pltpu.CompilerParams(vmem_limit_bytes=4 * 2**20),
        cost_estimate=pl.CostEstimate(flops=0, bytes_accessed=8 * 10**5, transcendentals=0),
        name="late_halo_rows",
    )(*blocks, *deps)


def dot_nt(a, b):
    return lax.dot_general(a, b, (((1,), (1,)), ((), ())), preferred_element_type=jnp.float32)


def dot_tn(a, b):
    return lax.dot_general(a, b, (((0,), (0,)), ((), ())), preferred_element_type=jnp.float32)


def attend_kernel(
    first_tile, last_tile, blocks, has_prev, late, scal, lam_ref, gain_ref, ends_ref, *refs
):
    recv = refs[:4] if late else refs[:1]
    refs = refs[len(recv):]
    prev_ref = refs[0] if has_prev else None
    refs = refs[1:] if has_prev else refs
    dq_ref, dkv_ref = refs[:2]
    back_ref = refs[2] if has_prev else None
    q_s, g_s, k_w, v_w, dk_s, dv_s = refs[-6:]
    lam = lam_ref[0]

    def place(index):
        if not late:
            return index * ROWS
        return pl.multiple_of(lax.rem(scal[0] + 4 - index, 4) * ROWS, ROWS)

    shift = first_tile * TILE
    for index in range(blocks):
        block = recv[index] if late else recv[0].at[PLACE[index]]
        if late or (index + 1) * ROWS > shift - SPAN and index * ROWS < last_tile * TILE:
            row = place(index)
            low = 0 if late else max(0, shift - SPAN - index * ROWS)
            high = ROWS if late else min(ROWS, last_tile * TILE - index * ROWS)
            k_w[pl.ds(SPAN + row + low - shift, high - low)] = block[0, low:high]
            v_w[pl.ds(SPAN + row + low - shift, high - low)] = block[1, low:high]
        if late or (index + 1) * ROWS > shift and index * ROWS < last_tile * TILE:
            row = place(index)
            low = 0 if late else max(0, shift - index * ROWS)
            high = ROWS if late else min(ROWS, last_tile * TILE - index * ROWS)
            q_s[pl.ds(row + low - shift, high - low)] = block[2, low:high]
            g_s[pl.ds(row + low - shift, high - low)] = block[3, low:high]
    if has_prev:
        for index in range(4):
            row = place(index)
            k_w[pl.ds(row, ROWS)] = prev_ref[index, 0]
            v_w[pl.ds(row, ROWS)] = prev_ref[index, 1]
    dk_s[...] = jnp.zeros_like(dk_s)
    dv_s[...] = jnp.zeros_like(dv_s)

    def tile(i, n):
        width = n * TILE
        row = pl.multiple_of(i * TILE, TILE)
        left = pl.multiple_of((4 + i - n) * TILE, TILE)
        rows, cols = pl.ds(row, TILE), pl.ds(left, width)
        k, v = k_w[cols], v_w[cols]
        first = lax.broadcasted_iota(jnp.int32, (TILE, HEAD_DIM), 1) < HEAD_DIM // 2
        q = q_s[rows].astype(jnp.float32) * score_scale
        q_two = jnp.concatenate(
            [jnp.where(first, q, 0.0), jnp.where(first, 0.0, q)], axis=0
        ).astype(jnp.bfloat16)
        scores = dot_nt(q_two, k)
        base = scal[1] + shift
        spot = lax.broadcasted_iota(jnp.int32, (TILE, width), 1) + (base - SPAN + left)
        own = lax.broadcasted_iota(jnp.int32, (TILE, width), 0) + (base + row)
        at = lax.broadcasted_iota(jnp.int32, (TILE, HEAD_DIM), 0) + (base + row)
        ends = ends_ref[...]
        begin = jnp.max(jnp.where(ends <= at, ends, 0), axis=1, keepdims=True)
        live = (spot >= begin) & (spot <= own)

        def soft(score):
            score = jnp.where(live, score, masked_value)
            raised = jnp.exp(score - jnp.max(score, axis=1, keepdims=True))
            return raised * (1.0 / jnp.sum(raised, axis=1, keepdims=True))

        prob_one, prob_two = soft(scores[:TILE]), soft(scores[TILE:])
        prob_one_b, prob_two_b = prob_one.astype(jnp.bfloat16), prob_two.astype(jnp.bfloat16)
        out_one = jnp.dot(prob_one_b, v, preferred_element_type=jnp.float32)
        out_two = jnp.dot(prob_two_b, v, preferred_element_type=jnp.float32)
        attended = out_one - lam * out_two
        scaled = g_s[rows].astype(jnp.float32) * gain_ref[...] * (1.0 - lambda_init)
        inv_rms = lax.rsqrt(jnp.mean(attended * attended, axis=1, keepdims=True) + norm_epsilon)
        d_att = inv_rms * scaled - attended * (inv_rms * inv_rms * inv_rms) * jnp.mean(
            attended * scaled, axis=1, keepdims=True
        )
        d_att_b = d_att.astype(jnp.bfloat16)
        delta_one = jnp.sum(d_att * out_one, axis=1, keepdims=True)
        delta_two = -lam * jnp.sum(d_att * out_two, axis=1, keepdims=True)
        grad_probs = dot_nt(d_att_b, v)
        ds_one = (prob_one * (grad_probs - delta_one)).astype(jnp.bfloat16)
        ds_two = (prob_two * (-lam * grad_probs - delta_two)).astype(jnp.bfloat16)
        dq_one = jnp.dot(ds_one, k, preferred_element_type=jnp.float32)
        dq_two = jnp.dot(ds_two, k, preferred_element_type=jnp.float32)
        dq_ref[rows] = (jnp.where(first, dq_one, dq_two) * score_scale).astype(jnp.bfloat16)
        dk_s[:, cols] += dot_tn(q_two, jnp.concatenate([ds_one, ds_two], axis=0))
        dv_s[:, cols] += dot_tn(d_att_b, prob_one_b) - lam * dot_tn(d_att_b, prob_two_b)

    def step(i, carry):
        tiles = scal[2 + first_tile + i]
        for n in range(1, 5):
            pl.when(tiles == n)(functools.partial(tile, i, n))
        return carry

    lax.fori_loop(0, last_tile - first_tile, step, 0)
    if has_prev:
        back_ref[0] = dk_s[:, :SPAN].T.astype(jnp.bfloat16)
        back_ref[1] = dv_s[:, :SPAN].T.astype(jnp.bfloat16)
        dkv_ref[0] = dk_s[:, SPAN:].T
        dkv_ref[1] = dv_s[:, SPAN:].T
    else:
        dkv_ref[0] = dk_s[...].T
        dkv_ref[1] = dv_s[...].T


def attend(name, tiles, scal, lam, gain, ends, recv, prev, deps=()):
    late = isinstance(recv, list)
    blocks = len(recv) if late else recv.shape[0]
    recv = recv if late else [recv]
    first_tile, last_tile = tiles
    queries = (last_tile - first_tile) * TILE
    window = queries + SPAN
    has_prev = prev is not None
    out_shape = [
        jax.ShapeDtypeStruct((queries, HEAD_DIM), jnp.bfloat16),
        jax.ShapeDtypeStruct((2, queries if has_prev else window, HEAD_DIM), jnp.float32),
    ]
    if has_prev:
        out_shape.append(jax.ShapeDtypeStruct((2, SPAN, HEAD_DIM), jnp.bfloat16))
    inputs = [scal, lam, gain, ends, *recv] + ([prev] if has_prev else [])
    body = functools.partial(attend_kernel, first_tile, last_tile, blocks, has_prev, late)
    count = last_tile - first_tile
    return pl.pallas_call(
        spread(body, len(inputs), deps),
        out_shape=out_shape,
        in_specs=[smem_spec] * 2 + [vmem_spec] * (len(inputs) - 2) + [any_spec] * len(deps),
        out_specs=[vmem_spec] * len(out_shape),
        scratch_shapes=[
            pltpu.VMEM((queries, HEAD_DIM), jnp.bfloat16),
            pltpu.VMEM((queries, HEAD_DIM), jnp.bfloat16),
            pltpu.VMEM((window, HEAD_DIM), jnp.bfloat16),
            pltpu.VMEM((window, HEAD_DIM), jnp.bfloat16),
            pltpu.VMEM((HEAD_DIM, window), jnp.float32),
            pltpu.VMEM((HEAD_DIM, window), jnp.float32),
        ],
        compiler_params=pltpu.CompilerParams(vmem_limit_bytes=36 * 2**20),
        cost_estimate=pl.CostEstimate(
            flops=count * 2 * 10**9, bytes_accessed=count * 10**6, transcendentals=count * 3 * 10**5
        ),
        name=name,
    )(*inputs, *deps)


def merge_column_kernel(dq_b, dkv_b, dq_a, dkv_a, dq_c, dkv_c, dq_d, dkv_d, halo_ref, out, dq_s, sum_s):
    dq_s[0:768] = dq_a[...]
    dq_s[768:1792] = dq_b[...]
    dq_s[1792:2304] = dq_c[...]
    dq_s[2304:3072] = dq_d[...]
    for a in range(2):
        sum_s[a, 0:768] = dkv_b[a, 0:768] + dkv_a[a]
        sum_s[a, 768:1024] = dkv_b[a, 768:1024]
        sum_s[a, 1024:1536] = dkv_b[a, 1024:1536] + dkv_c[a, 0:512]
        sum_s[a, 1536:1792] = dkv_b[a, 1536:1792] + dkv_c[a, 512:768] + dkv_d[a, 0:256]
        sum_s[a, 1792:2304] = dkv_c[a, 768:1280] + dkv_d[a, 256:768]
        sum_s[a, 2304:3072] = dkv_d[a, 768:1536] + halo_ref[a].astype(jnp.float32)
    for block in range(COLUMN):
        rows, b = slice(block * ROWS, (block + 1) * ROWS), PLACE[block]
        out[b, 0] = dq_s[rows]
        out[b, 1] = sum_s[0, rows].astype(jnp.bfloat16)
        out[b, 2] = sum_s[1, rows].astype(jnp.bfloat16)


def merge_column(parts, halo, deps=()):
    run = COLUMN * ROWS
    return pl.pallas_call(
        spread(merge_column_kernel, 9, deps),
        out_shape=jax.ShapeDtypeStruct((COLUMN, 3, ROWS, HEAD_DIM), jnp.bfloat16),
        in_specs=[vmem_spec] * 9 + [any_spec] * len(deps),
        out_specs=vmem_spec,
        scratch_shapes=[
            pltpu.VMEM((run, HEAD_DIM), jnp.bfloat16),
            pltpu.VMEM((2, run, HEAD_DIM), jnp.float32),
        ],
        compiler_params=pltpu.CompilerParams(vmem_limit_bytes=24 * 2**20),
        cost_estimate=pl.CostEstimate(flops=0, bytes_accessed=8 * 10**6, transcendentals=0),
        name="merge_column",
    )(*parts, halo, *deps)


def merge_late_kernel(hp_ref, dq_ref, dkv_ref, halo_ref, *outs):
    for k, out in enumerate(outs):
        rows = pl.ds(pl.multiple_of(lax.rem(hp_ref[0] + 4 - k, 4) * ROWS, ROWS), ROWS)
        out[0] = dq_ref[rows]
        for a in range(2):
            out[1 + a] = (dkv_ref[a, rows] + halo_ref[a, rows].astype(jnp.float32)).astype(
                jnp.bfloat16
            )


def merge_late(hp, dq, dkv, halo, deps=()):
    return pl.pallas_call(
        spread(merge_late_kernel, 4, deps),
        out_shape=[jax.ShapeDtypeStruct((3, ROWS, HEAD_DIM), jnp.bfloat16)] * 4,
        in_specs=[smem_spec] + [vmem_spec] * 3 + [any_spec] * len(deps),
        out_specs=[vmem_spec] * 4,
        compiler_params=pltpu.CompilerParams(vmem_limit_bytes=8 * 2**20),
        cost_estimate=pl.CostEstimate(flops=0, bytes_accessed=2 * 10**6, transcendentals=0),
        name="merge_late",
    )(hp, dq, dkv, halo, *deps)


def unpack_kernel(hp_ref, col_ref, l0, l1, l2, l3, *rest):
    outs, sem = rest[:3], rest[3]
    pairs = [
        (col_ref.at[h, a], outs[a].at[:, columns(h)]) for a in range(3) for h in range(COLUMN)
    ]
    for k, src in enumerate((l0, l1, l2, l3)):
        cols = columns(COLUMN + lax.rem(hp_ref[0] + k, 4))
        pairs += [(src.at[a], outs[a].at[:, cols]) for a in range(3)]
    run_copies(pairs, sem)


def unpack(hp, column, late, width):
    return pl.pallas_call(
        unpack_kernel,
        out_shape=[jax.ShapeDtypeStruct((ROWS, width), jnp.bfloat16)] * 3,
        in_specs=[smem_spec] + [any_spec] * 5,
        out_specs=[any_spec] * 3,
        scratch_shapes=[pltpu.SemaphoreType.DMA((60,))],
        compiler_params=pltpu.CompilerParams(vmem_limit_bytes=4 * 2**20),
        name="unpack",
    )(hp, column, *late)


def per_device(queries, keys, values, grad_out, lambdas, norm_gain, doc_lengths):
    col, z_lo, core, hp = (lax.axis_index(a) for a in AXES)
    hp_s = hp[None].astype(jnp.int32)
    doc_ends = jnp.cumsum(doc_lengths)
    ends = doc_ends[None, :]
    gain = norm_gain[None, :]

    def scalars(start, tiles):
        at = start + TILE * jnp.arange(tiles, dtype=jnp.int32)
        begin = jnp.max(jnp.where(ends <= at[:, None], ends, 0), axis=1)
        count = 4 + jnp.arange(tiles, dtype=jnp.int32) - (begin - (start - SPAN)) // TILE
        return jnp.concatenate([hp_s, start[None], count]).astype(jnp.int32)

    column_scal = scalars(col * (COLUMN * ROWS), 12)
    late_scal = scalars((col * 4 + z_lo * 2 + core) * SPAN, 3)
    column_lam = lax.dynamic_slice_in_dim(lambdas, core * 8 + z_lo * 4 + hp, 1)
    late_lam = lax.dynamic_slice_in_dim(lambdas, COLUMN + hp, 1)
    arrays = (keys, values, queries, grad_out)

    chunk = [(d, d + 4) for d in range(252)]
    run = [(d, d + 16) for d in range(240)]
    turn = [[(d, d // 4 * 4 + (d + k) % 4) for d in range(256)] for k in range(4)]

    def back(route):
        return [(b, a) for a, b in route]

    def send(block, route):
        return lax.ppermute(block, AXES, route)

    packed = pack_column(arrays)
    recv = lax.all_to_all(packed, RING, split_axis=0, concat_axis=0, tiled=True)
    late_sent = pack_late(hp_s, arrays, (packed,))
    late_recv = [late_sent[0]] + [send(late_sent[k], turn[k]) for k in range(1, 4)]
    prev = send(recv[12:, :2], run)

    b_part = attend("attend_b", (3, 7), column_scal, column_lam, gain, ends, recv, None, (late_sent[0],))
    late_prev = send(late_halo_rows(late_recv, (b_part[0],)), chunk)
    a_part = attend("attend_a", (0, 3), column_scal, column_lam, gain, ends, recv, prev, (b_part[0],))
    halo = send(a_part[2], back(run))
    late_part = attend(
        "attend_late", (0, 3), late_scal, late_lam, gain, ends, late_recv, late_prev, (a_part[0],)
    )
    late_halo = send(late_part[2], back(chunk))
    c_part = attend("attend_c", (7, 9), column_scal, column_lam, gain, ends, recv, None, (late_part[0],))
    late_merged = merge_late(hp_s, late_part[0], late_part[1], late_halo, (c_part[0],))
    late = [late_merged[0]] + [send(late_merged[k], back(turn[k])) for k in range(1, 4)]
    d_part = attend("attend_d", (9, 12), column_scal, column_lam, gain, ends, recv, None, (late_merged[0],))
    merged = merge_column((*b_part, *a_part[:2], *c_part, *d_part), halo, tuple(late[1:]))
    column = lax.all_to_all(merged, RING, split_axis=0, concat_axis=0, tiled=True)
    return tuple(unpack(hp_s, column, late, queries.shape[1]))


def solution(mesh):
    grid = Mesh(mesh.devices.reshape(16, 2, 2, 4), AXES)
    spec = P(AXES, None)
    return jax.shard_map(
        per_device,
        mesh=grid,
        in_specs=(spec,) * 4 + (P(),) * 3,
        out_specs=(spec,) * 3,
        check_vma=False,
    )
```

```python
import functools

import jax
import jax.numpy as jnp
from jax import lax
from jax.experimental import pallas as pl
from jax.experimental.pallas import tpu as pltpu
from jax.sharding import Mesh, PartitionSpec as P

HEAD_DIM = 128
SPAN = 768
ROWS = 192
TILE = 256
COLUMN = 16
LATE = 4
score_scale = 0.125
norm_epsilon = 1e-05
lambda_init = 0.8
masked_value = -1e30
AXES = ("col", "z_lo", "core", "hp")
RING = ("core", "z_lo", "hp")

PLACE = [(b // 4 % 2 * 2 + b // 8) * 4 + b % 4 for b in range(COLUMN)]

any_spec = pl.BlockSpec(memory_space=pl.ANY)
smem_spec = pl.BlockSpec(memory_space=pltpu.SMEM)
vmem_spec = pl.BlockSpec(memory_space=pltpu.VMEM)


def spread(kernel, inputs, deps):
    def ordered(*refs):
        kernel(*refs[:inputs], *refs[inputs + len(deps):])

    return ordered


def run_copies(pairs, sem):
    copies = [pltpu.make_async_copy(a, b, sem.at[i]) for i, (a, b) in enumerate(pairs)]
    for copy in copies:
        copy.start()
    for copy in copies:
        copy.wait()


def columns(head):
    start = head * HEAD_DIM
    return pl.ds(start if isinstance(head, int) else pl.multiple_of(start, HEAD_DIM), HEAD_DIM)


def pack_kernel(part, src, *refs):
    out, sem = refs[-2:]
    run_copies([(src.at[:, columns(h)], out.at[h, part]) for h in range(COLUMN)], sem)


def pack_column(arrays, deps):
    shape = jax.ShapeDtypeStruct((COLUMN, 4, ROWS, HEAD_DIM), jnp.bfloat16)
    out = None
    for part, array in enumerate(arrays):
        inputs = [array] if out is None else [array, out]
        out = pl.pallas_call(
            functools.partial(pack_kernel, part),
            out_shape=shape,
            in_specs=[any_spec] * len(inputs),
            out_specs=any_spec,
            scratch_shapes=[pltpu.SemaphoreType.DMA((COLUMN,))],
            input_output_aliases={} if out is None else {1: 0},
            compiler_params=pltpu.CompilerParams(vmem_limit_bytes=4 * 2**20),
            cost_estimate=pl.CostEstimate(flops=0, bytes_accessed=15 * 10**5, transcendentals=0),
            name="pack_column",
        )(*inputs)
    return out


def pack_late_kernel(hp_ref, k_ref, v_ref, q_ref, g_ref, *rest):
    outs, sem = rest[:4], rest[4]
    run_copies(
        [
            (src.at[:, columns(COLUMN + lax.rem(hp_ref[0] + k, 4))], outs[k].at[a])
            for k in range(4)
            for a, src in enumerate((k_ref, v_ref, q_ref, g_ref))
        ],
        sem,
    )


def pack_late(hp, arrays, deps):
    return pl.pallas_call(
        spread(pack_late_kernel, 5, deps),
        out_shape=[jax.ShapeDtypeStruct((4, ROWS, HEAD_DIM), jnp.bfloat16)] * 4,
        in_specs=[smem_spec] + [any_spec] * (4 + len(deps)),
        out_specs=[any_spec] * 4,
        scratch_shapes=[pltpu.SemaphoreType.DMA((16,))],
        compiler_params=pltpu.CompilerParams(vmem_limit_bytes=4 * 2**20),
        cost_estimate=pl.CostEstimate(flops=0, bytes_accessed=16 * 10**5, transcendentals=0),
        name="pack_late",
    )(hp, *arrays, *deps)


def halo_kernel(l0, l1, l2, l3, out, sem):
    run_copies([(src.at[pl.ds(0, 2)], out.at[k]) for k, src in enumerate((l0, l1, l2, l3))], sem)


def late_halo_rows(blocks, deps):
    return pl.pallas_call(
        spread(halo_kernel, 4, deps),
        out_shape=jax.ShapeDtypeStruct((4, 2, ROWS, HEAD_DIM), jnp.bfloat16),
        in_specs=[any_spec] * (4 + len(deps)),
        out_specs=any_spec,
        scratch_shapes=[pltpu.SemaphoreType.DMA((4,))],
        compiler_params=pltpu.CompilerParams(vmem_limit_bytes=4 * 2**20),
        cost_estimate=pl.CostEstimate(flops=0, bytes_accessed=8 * 10**5, transcendentals=0),
        name="late_halo_rows",
    )(*blocks, *deps)


def dot_nt(a, b):
    return lax.dot_general(a, b, (((1,), (1,)), ((), ())), preferred_element_type=jnp.float32)


def dot_tn(a, b):
    return lax.dot_general(a, b, (((0,), (0,)), ((), ())), preferred_element_type=jnp.float32)


def attend_kernel(
    first_tile, last_tile, blocks, has_prev, late, scal, lam_ref, gain_ref, ends_ref, *refs
):
    recv = refs[:4] if late else refs[:1]
    refs = refs[len(recv):]
    prev_ref = refs[0] if has_prev else None
    refs = refs[1:] if has_prev else refs
    dq_ref, dkv_ref = refs[:2]
    back_ref = refs[2] if has_prev else None
    q_s, g_s, k_w, v_w, dk_s, dv_s = refs[-6:]
    lam = lam_ref[0]

    def place(index):
        if not late:
            return index * ROWS
        return pl.multiple_of(lax.rem(scal[0] + 4 - index, 4) * ROWS, ROWS)

    shift = first_tile * TILE
    for index in range(blocks):
        block = recv[index] if late else recv[0].at[PLACE[index]]
        if late or (index + 1) * ROWS > shift - SPAN and index * ROWS < last_tile * TILE:
            row = place(index)
            low = 0 if late else max(0, shift - SPAN - index * ROWS)
            high = ROWS if late else min(ROWS, last_tile * TILE - index * ROWS)
            k_w[pl.ds(SPAN + row + low - shift, high - low)] = block[0, low:high]
            v_w[pl.ds(SPAN + row + low - shift, high - low)] = block[1, low:high]
        if late or (index + 1) * ROWS > shift and index * ROWS < last_tile * TILE:
            row = place(index)
            low = 0 if late else max(0, shift - index * ROWS)
            high = ROWS if late else min(ROWS, last_tile * TILE - index * ROWS)
            q_s[pl.ds(row + low - shift, high - low)] = block[2, low:high]
            g_s[pl.ds(row + low - shift, high - low)] = block[3, low:high]
    if has_prev:
        for index in range(4):
            row = place(index)
            k_w[pl.ds(row, ROWS)] = prev_ref[index, 0]
            v_w[pl.ds(row, ROWS)] = prev_ref[index, 1]
    dk_s[...] = jnp.zeros_like(dk_s)
    dv_s[...] = jnp.zeros_like(dv_s)

    def tile(i, n):
        width = n * TILE
        row = pl.multiple_of(i * TILE, TILE)
        left = pl.multiple_of((4 + i - n) * TILE, TILE)
        rows, cols = pl.ds(row, TILE), pl.ds(left, width)
        k, v = k_w[cols], v_w[cols]
        first = lax.broadcasted_iota(jnp.int32, (TILE, HEAD_DIM), 1) < HEAD_DIM // 2
        q = q_s[rows].astype(jnp.float32) * score_scale
        q_two = jnp.concatenate(
            [jnp.where(first, q, 0.0), jnp.where(first, 0.0, q)], axis=0
        ).astype(jnp.bfloat16)
        scores = dot_nt(q_two, k)
        base = scal[1] + shift
        spot = lax.broadcasted_iota(jnp.int32, (TILE, width), 1) + (base - SPAN + left)
        own = lax.broadcasted_iota(jnp.int32, (TILE, width), 0) + (base + row)
        at = lax.broadcasted_iota(jnp.int32, (TILE, HEAD_DIM), 0) + (base + row)
        ends = ends_ref[...]
        begin = jnp.max(jnp.where(ends <= at, ends, 0), axis=1, keepdims=True)
        live = (spot >= begin) & (spot <= own)

        def soft(score):
            score = jnp.where(live, score, masked_value)
            raised = jnp.exp(score - jnp.max(score, axis=1, keepdims=True))
            return raised * (1.0 / jnp.sum(raised, axis=1, keepdims=True))

        prob_one, prob_two = soft(scores[:TILE]), soft(scores[TILE:])
        prob_one_b, prob_two_b = prob_one.astype(jnp.bfloat16), prob_two.astype(jnp.bfloat16)
        out_one = jnp.dot(prob_one_b, v, preferred_element_type=jnp.float32)
        out_two = jnp.dot(prob_two_b, v, preferred_element_type=jnp.float32)
        attended = out_one - lam * out_two
        scaled = g_s[rows].astype(jnp.float32) * gain_ref[...] * (1.0 - lambda_init)
        inv_rms = lax.rsqrt(jnp.mean(attended * attended, axis=1, keepdims=True) + norm_epsilon)
        d_att = inv_rms * scaled - attended * (inv_rms * inv_rms * inv_rms) * jnp.mean(
            attended * scaled, axis=1, keepdims=True
        )
        d_att_b = d_att.astype(jnp.bfloat16)
        delta_one = jnp.sum(d_att * out_one, axis=1, keepdims=True)
        delta_two = -lam * jnp.sum(d_att * out_two, axis=1, keepdims=True)
        grad_probs = dot_nt(d_att_b, v)
        ds_one = (prob_one * (grad_probs - delta_one)).astype(jnp.bfloat16)
        ds_two = (prob_two * (-lam * grad_probs - delta_two)).astype(jnp.bfloat16)
        dq_one = jnp.dot(ds_one, k, preferred_element_type=jnp.float32)
        dq_two = jnp.dot(ds_two, k, preferred_element_type=jnp.float32)
        dq_ref[rows] = (jnp.where(first, dq_one, dq_two) * score_scale).astype(jnp.bfloat16)
        dk_s[:, cols] += dot_tn(q_two, jnp.concatenate([ds_one, ds_two], axis=0))
        dv_s[:, cols] += dot_tn(d_att_b, prob_one_b) - lam * dot_tn(d_att_b, prob_two_b)

    def step(i, carry):
        tiles = scal[2 + first_tile + i]
        for n in range(1, 5):
            pl.when(tiles == n)(functools.partial(tile, i, n))
        return carry

    lax.fori_loop(0, last_tile - first_tile, step, 0)
    if has_prev:
        back_ref[0] = dk_s[:, :SPAN].T.astype(jnp.bfloat16)
        back_ref[1] = dv_s[:, :SPAN].T.astype(jnp.bfloat16)
        dkv_ref[0] = dk_s[:, SPAN:].T
        dkv_ref[1] = dv_s[:, SPAN:].T
    else:
        dkv_ref[0] = dk_s[...].T
        dkv_ref[1] = dv_s[...].T


def attend(name, tiles, scal, lam, gain, ends, recv, prev, deps=()):
    late = isinstance(recv, list)
    blocks = len(recv) if late else recv.shape[0]
    recv = recv if late else [recv]
    first_tile, last_tile = tiles
    queries = (last_tile - first_tile) * TILE
    window = queries + SPAN
    has_prev = prev is not None
    out_shape = [
        jax.ShapeDtypeStruct((queries, HEAD_DIM), jnp.bfloat16),
        jax.ShapeDtypeStruct((2, queries if has_prev else window, HEAD_DIM), jnp.float32),
    ]
    if has_prev:
        out_shape.append(jax.ShapeDtypeStruct((2, SPAN, HEAD_DIM), jnp.bfloat16))
    inputs = [scal, lam, gain, ends, *recv] + ([prev] if has_prev else [])
    body = functools.partial(attend_kernel, first_tile, last_tile, blocks, has_prev, late)
    count = last_tile - first_tile
    return pl.pallas_call(
        spread(body, len(inputs), deps),
        out_shape=out_shape,
        in_specs=[smem_spec] * 2 + [vmem_spec] * (len(inputs) - 2) + [any_spec] * len(deps),
        out_specs=[vmem_spec] * len(out_shape),
        scratch_shapes=[
            pltpu.VMEM((queries, HEAD_DIM), jnp.bfloat16),
            pltpu.VMEM((queries, HEAD_DIM), jnp.bfloat16),
            pltpu.VMEM((window, HEAD_DIM), jnp.bfloat16),
            pltpu.VMEM((window, HEAD_DIM), jnp.bfloat16),
            pltpu.VMEM((HEAD_DIM, window), jnp.float32),
            pltpu.VMEM((HEAD_DIM, window), jnp.float32),
        ],
        compiler_params=pltpu.CompilerParams(vmem_limit_bytes=36 * 2**20),
        cost_estimate=pl.CostEstimate(
            flops=count * 2 * 10**9, bytes_accessed=count * 10**6, transcendentals=count * 3 * 10**5
        ),
        name=name,
    )(*inputs, *deps)


def merge_column_kernel(dq_b, dkv_b, dq_a, dkv_a, dq_c, dkv_c, dq_d, dkv_d, halo_ref, out, dq_s, sum_s):
    dq_s[0:768] = dq_a[...]
    dq_s[768:1792] = dq_b[...]
    dq_s[1792:2304] = dq_c[...]
    dq_s[2304:3072] = dq_d[...]
    for a in range(2):
        sum_s[a, 0:768] = dkv_b[a, 0:768] + dkv_a[a]
        sum_s[a, 768:1024] = dkv_b[a, 768:1024]
        sum_s[a, 1024:1536] = dkv_b[a, 1024:1536] + dkv_c[a, 0:512]
        sum_s[a, 1536:1792] = dkv_b[a, 1536:1792] + dkv_c[a, 512:768] + dkv_d[a, 0:256]
        sum_s[a, 1792:2304] = dkv_c[a, 768:1280] + dkv_d[a, 256:768]
        sum_s[a, 2304:3072] = dkv_d[a, 768:1536] + halo_ref[a].astype(jnp.float32)
    for block in range(COLUMN):
        rows, b = slice(block * ROWS, (block + 1) * ROWS), PLACE[block]
        out[b, 0] = dq_s[rows]
        out[b, 1] = sum_s[0, rows].astype(jnp.bfloat16)
        out[b, 2] = sum_s[1, rows].astype(jnp.bfloat16)


def merge_column(parts, halo, deps=()):
    run = COLUMN * ROWS
    return pl.pallas_call(
        spread(merge_column_kernel, 9, deps),
        out_shape=jax.ShapeDtypeStruct((COLUMN, 3, ROWS, HEAD_DIM), jnp.bfloat16),
        in_specs=[vmem_spec] * 9 + [any_spec] * len(deps),
        out_specs=vmem_spec,
        scratch_shapes=[
            pltpu.VMEM((run, HEAD_DIM), jnp.bfloat16),
            pltpu.VMEM((2, run, HEAD_DIM), jnp.float32),
        ],
        compiler_params=pltpu.CompilerParams(vmem_limit_bytes=24 * 2**20),
        cost_estimate=pl.CostEstimate(flops=0, bytes_accessed=8 * 10**6, transcendentals=0),
        name="merge_column",
    )(*parts, halo, *deps)


def merge_late_kernel(hp_ref, dq_ref, dkv_ref, halo_ref, *outs):
    for k, out in enumerate(outs):
        rows = pl.ds(pl.multiple_of(lax.rem(hp_ref[0] + 4 - k, 4) * ROWS, ROWS), ROWS)
        out[0] = dq_ref[rows]
        for a in range(2):
            out[1 + a] = (dkv_ref[a, rows] + halo_ref[a, rows].astype(jnp.float32)).astype(
                jnp.bfloat16
            )


def merge_late(hp, dq, dkv, halo, deps=()):
    return pl.pallas_call(
        spread(merge_late_kernel, 4, deps),
        out_shape=[jax.ShapeDtypeStruct((3, ROWS, HEAD_DIM), jnp.bfloat16)] * 4,
        in_specs=[smem_spec] + [vmem_spec] * 3 + [any_spec] * len(deps),
        out_specs=[vmem_spec] * 4,
        compiler_params=pltpu.CompilerParams(vmem_limit_bytes=8 * 2**20),
        cost_estimate=pl.CostEstimate(flops=0, bytes_accessed=2 * 10**6, transcendentals=0),
        name="merge_late",
    )(hp, dq, dkv, halo, *deps)


def unpack_kernel(hp_ref, col_ref, l0, l1, l2, l3, *rest):
    outs, sem = rest[:3], rest[3]
    pairs = [
        (col_ref.at[h, a], outs[a].at[:, columns(h)]) for a in range(3) for h in range(COLUMN)
    ]
    for k, src in enumerate((l0, l1, l2, l3)):
        cols = columns(COLUMN + lax.rem(hp_ref[0] + k, 4))
        pairs += [(src.at[a], outs[a].at[:, cols]) for a in range(3)]
    run_copies(pairs, sem)


def unpack(hp, column, late, width):
    return pl.pallas_call(
        unpack_kernel,
        out_shape=[jax.ShapeDtypeStruct((ROWS, width), jnp.bfloat16)] * 3,
        in_specs=[smem_spec] + [any_spec] * 5,
        out_specs=[any_spec] * 3,
        scratch_shapes=[pltpu.SemaphoreType.DMA((60,))],
        compiler_params=pltpu.CompilerParams(vmem_limit_bytes=4 * 2**20),
        name="unpack",
    )(hp, column, *late)


def per_device(queries, keys, values, grad_out, lambdas, norm_gain, doc_lengths):
    col, z_lo, core, hp = (lax.axis_index(a) for a in AXES)
    hp_s = hp[None].astype(jnp.int32)
    doc_ends = jnp.cumsum(doc_lengths)
    ends = doc_ends[None, :]
    gain = norm_gain[None, :]

    def scalars(start, tiles):
        at = start + TILE * jnp.arange(tiles, dtype=jnp.int32)
        begin = jnp.max(jnp.where(ends <= at[:, None], ends, 0), axis=1)
        count = 4 + jnp.arange(tiles, dtype=jnp.int32) - (begin - (start - SPAN)) // TILE
        return jnp.concatenate([hp_s, start[None], count]).astype(jnp.int32)

    column_scal = scalars(col * (COLUMN * ROWS), 12)
    late_scal = scalars((col * 4 + z_lo * 2 + core) * SPAN, 3)
    column_lam = lax.dynamic_slice_in_dim(lambdas, core * 8 + z_lo * 4 + hp, 1)
    late_lam = lax.dynamic_slice_in_dim(lambdas, COLUMN + hp, 1)
    arrays = (keys, values, queries, grad_out)

    chunk = [(d, d + 4) for d in range(252)]
    run = [(d, d + 16) for d in range(240)]
    turn = [[(d, d // 4 * 4 + (d + k) % 4) for d in range(256)] for k in range(4)]

    def back(route):
        return [(b, a) for a, b in route]

    def send(block, route):
        return lax.ppermute(block, AXES, route)

    packed = pack_column(arrays, ())
    recv = lax.all_to_all(packed, RING, split_axis=0, concat_axis=0, tiled=True)
    late_sent = pack_late(hp_s, arrays, (packed,))
    late_recv = [late_sent[0]] + [send(late_sent[k], turn[k]) for k in range(1, 4)]
    prev = send(recv[12:, :2], run)

    b_part = attend("attend_b", (3, 7), column_scal, column_lam, gain, ends, recv, None, (late_sent[0],))
    late_prev = send(late_halo_rows(late_recv, (b_part[0],)), chunk)
    a_part = attend("attend_a", (0, 3), column_scal, column_lam, gain, ends, recv, prev, (b_part[0],))
    halo = send(a_part[2], back(run))
    late_part = attend(
        "attend_late", (0, 3), late_scal, late_lam, gain, ends, late_recv, late_prev, (a_part[0],)
    )
    late_halo = send(late_part[2], back(chunk))
    c_part = attend("attend_c", (7, 9), column_scal, column_lam, gain, ends, recv, None, (late_part[0],))
    late_merged = merge_late(hp_s, late_part[0], late_part[1], late_halo, (c_part[0],))
    late = [late_merged[0]] + [send(late_merged[k], back(turn[k])) for k in range(1, 4)]
    d_part = attend("attend_d", (9, 12), column_scal, column_lam, gain, ends, recv, None, (late_merged[0],))
    merged = merge_column((*b_part, *a_part[:2], *c_part, *d_part), halo, tuple(late[1:]))
    column = lax.all_to_all(merged, RING, split_axis=0, concat_axis=0, tiled=True)
    return tuple(unpack(hp_s, column, late, queries.shape[1]))


def solution(mesh):
    grid = Mesh(mesh.devices.reshape(16, 2, 2, 4), AXES)
    spec = P(AXES, None)
    return jax.shard_map(
        per_device,
        mesh=grid,
        in_specs=(spec,) * 4 + (P(),) * 3,
        out_specs=(spec,) * 3,
        check_vma=False,
    )
```

```python
import functools

import jax
import jax.numpy as jnp
from jax import lax
from jax.experimental import pallas as pl
from jax.experimental.pallas import tpu as pltpu
from jax.sharding import Mesh, PartitionSpec as P

HEAD_DIM = 128
SPAN = 768
ROWS = 192
TILE = 256
COLUMN = 16
LATE = 4
score_scale = 0.125
norm_epsilon = 1e-05
lambda_init = 0.8
masked_value = -1e30
AXES = ("col", "z_lo", "core", "hp")
RING = ("core", "z_lo", "hp")

PLACE = [(b // 4 % 2 * 2 + b // 8) * 4 + b % 4 for b in range(COLUMN)]

any_spec = pl.BlockSpec(memory_space=pl.ANY)
smem_spec = pl.BlockSpec(memory_space=pltpu.SMEM)
vmem_spec = pl.BlockSpec(memory_space=pltpu.VMEM)


def spread(kernel, inputs, deps):
    def ordered(*refs):
        kernel(*refs[:inputs], *refs[inputs + len(deps):])

    return ordered


def run_copies(pairs, sem):
    copies = [pltpu.make_async_copy(a, b, sem.at[i]) for i, (a, b) in enumerate(pairs)]
    for copy in copies:
        copy.start()
    for copy in copies:
        copy.wait()


def columns(head):
    start = head * HEAD_DIM
    return pl.ds(start if isinstance(head, int) else pl.multiple_of(start, HEAD_DIM), HEAD_DIM)


def pack_kernel(part, src, *refs):
    out, sem = refs[-2:]
    run_copies([(src.at[:, columns(h)], out.at[h, part]) for h in range(COLUMN)], sem)


def pack_column(arrays, deps):
    shape = jax.ShapeDtypeStruct((COLUMN, 4, ROWS, HEAD_DIM), jnp.bfloat16)
    out = None
    for part, array in enumerate(arrays):
        inputs = [array] if out is None else [array, out]
        out = pl.pallas_call(
            functools.partial(pack_kernel, part),
            out_shape=shape,
            in_specs=[any_spec] * len(inputs),
            out_specs=any_spec,
            scratch_shapes=[pltpu.SemaphoreType.DMA((COLUMN,))],
            input_output_aliases={} if out is None else {1: 0},
            compiler_params=pltpu.CompilerParams(vmem_limit_bytes=4 * 2**20),
            cost_estimate=pl.CostEstimate(flops=0, bytes_accessed=15 * 10**5, transcendentals=0),
            name="pack_column",
        )(*inputs)
    return out


def pack_late_kernel(hp_ref, k_ref, v_ref, q_ref, g_ref, *rest):
    outs, sem = rest[:4], rest[4]
    run_copies(
        [
            (src.at[:, columns(COLUMN + lax.rem(hp_ref[0] + k, 4))], outs[k].at[a])
            for k in range(4)
            for a, src in enumerate((k_ref, v_ref, q_ref, g_ref))
        ],
        sem,
    )


def pack_late(hp, arrays, deps):
    return pl.pallas_call(
        spread(pack_late_kernel, 5, deps),
        out_shape=[jax.ShapeDtypeStruct((4, ROWS, HEAD_DIM), jnp.bfloat16)] * 4,
        in_specs=[smem_spec] + [any_spec] * (4 + len(deps)),
        out_specs=[any_spec] * 4,
        scratch_shapes=[pltpu.SemaphoreType.DMA((16,))],
        compiler_params=pltpu.CompilerParams(vmem_limit_bytes=4 * 2**20),
        cost_estimate=pl.CostEstimate(flops=0, bytes_accessed=16 * 10**5, transcendentals=0),
        name="pack_late",
    )(hp, *arrays, *deps)


def halo_kernel(l0, l1, l2, l3, out, sem):
    run_copies([(src.at[pl.ds(0, 2)], out.at[k]) for k, src in enumerate((l0, l1, l2, l3))], sem)


def late_halo_rows(blocks, deps):
    return pl.pallas_call(
        spread(halo_kernel, 4, deps),
        out_shape=jax.ShapeDtypeStruct((4, 2, ROWS, HEAD_DIM), jnp.bfloat16),
        in_specs=[any_spec] * (4 + len(deps)),
        out_specs=any_spec,
        scratch_shapes=[pltpu.SemaphoreType.DMA((4,))],
        compiler_params=pltpu.CompilerParams(vmem_limit_bytes=4 * 2**20),
        cost_estimate=pl.CostEstimate(flops=0, bytes_accessed=8 * 10**5, transcendentals=0),
        name="late_halo_rows",
    )(*blocks, *deps)


def dot_nt(a, b):
    return lax.dot_general(a, b, (((1,), (1,)), ((), ())), preferred_element_type=jnp.float32)


def dot_tn(a, b):
    return lax.dot_general(a, b, (((0,), (0,)), ((), ())), preferred_element_type=jnp.float32)


def attend_kernel(
    first_tile, last_tile, blocks, has_prev, late, scal, lam_ref, gain_ref, ends_ref, *refs
):
    recv = refs[:4] if late else refs[:1]
    refs = refs[len(recv):]
    prev_ref = refs[0] if has_prev else None
    refs = refs[1:] if has_prev else refs
    dq_ref, dkv_ref = refs[:2]
    back_ref = refs[2] if has_prev else None
    q_s, g_s, k_w, v_w, dk_s, dv_s = refs[-6:]
    lam = lam_ref[0]

    def place(index):
        if not late:
            return index * ROWS
        return pl.multiple_of(lax.rem(scal[0] + 4 - index, 4) * ROWS, ROWS)

    shift = first_tile * TILE
    for index in range(blocks):
        block = recv[index] if late else recv[0].at[PLACE[index]]
        if late or (index + 1) * ROWS > shift - SPAN and index * ROWS < last_tile * TILE:
            row = place(index)
            low = 0 if late else max(0, shift - SPAN - index * ROWS)
            high = ROWS if late else min(ROWS, last_tile * TILE - index * ROWS)
            k_w[pl.ds(SPAN + row + low - shift, high - low)] = block[0, low:high]
            v_w[pl.ds(SPAN + row + low - shift, high - low)] = block[1, low:high]
        if late or (index + 1) * ROWS > shift and index * ROWS < last_tile * TILE:
            row = place(index)
            low = 0 if late else max(0, shift - index * ROWS)
            high = ROWS if late else min(ROWS, last_tile * TILE - index * ROWS)
            q_s[pl.ds(row + low - shift, high - low)] = block[2, low:high]
            g_s[pl.ds(row + low - shift, high - low)] = block[3, low:high]
    if has_prev:
        for index in range(4):
            row = place(index)
            k_w[pl.ds(row, ROWS)] = prev_ref[index, 0]
            v_w[pl.ds(row, ROWS)] = prev_ref[index, 1]
    dk_s[...] = jnp.zeros_like(dk_s)
    dv_s[...] = jnp.zeros_like(dv_s)

    def tile(i, n):
        width = n * TILE
        row = pl.multiple_of(i * TILE, TILE)
        left = pl.multiple_of((4 + i - n) * TILE, TILE)
        rows, cols = pl.ds(row, TILE), pl.ds(left, width)
        k, v = k_w[cols], v_w[cols]
        first = lax.broadcasted_iota(jnp.int32, (TILE, HEAD_DIM), 1) < HEAD_DIM // 2
        q = q_s[rows].astype(jnp.float32) * score_scale
        q_two = jnp.concatenate(
            [jnp.where(first, q, 0.0), jnp.where(first, 0.0, q)], axis=0
        ).astype(jnp.bfloat16)
        scores = dot_nt(q_two, k)
        base = scal[1] + shift
        spot = lax.broadcasted_iota(jnp.int32, (TILE, width), 1) + (base - SPAN + left)
        own = lax.broadcasted_iota(jnp.int32, (TILE, width), 0) + (base + row)
        at = lax.broadcasted_iota(jnp.int32, (TILE, HEAD_DIM), 0) + (base + row)
        ends = ends_ref[...]
        begin = jnp.max(jnp.where(ends <= at, ends, 0), axis=1, keepdims=True)
        live = (spot >= begin) & (spot <= own)

        def soft(score):
            score = jnp.where(live, score, masked_value)
            raised = jnp.exp(score - jnp.max(score, axis=1, keepdims=True))
            return raised * (1.0 / jnp.sum(raised, axis=1, keepdims=True))

        prob_one, prob_two = soft(scores[:TILE]), soft(scores[TILE:])
        prob_one_b, prob_two_b = prob_one.astype(jnp.bfloat16), prob_two.astype(jnp.bfloat16)
        out_one = jnp.dot(prob_one_b, v, preferred_element_type=jnp.float32)
        out_two = jnp.dot(prob_two_b, v, preferred_element_type=jnp.float32)
        attended = out_one - lam * out_two
        scaled = g_s[rows].astype(jnp.float32) * gain_ref[...] * (1.0 - lambda_init)
        inv_rms = lax.rsqrt(jnp.mean(attended * attended, axis=1, keepdims=True) + norm_epsilon)
        d_att = inv_rms * scaled - attended * (inv_rms * inv_rms * inv_rms) * jnp.mean(
            attended * scaled, axis=1, keepdims=True
        )
        d_att_b = d_att.astype(jnp.bfloat16)
        delta_one = jnp.sum(d_att * out_one, axis=1, keepdims=True)
        delta_two = -lam * jnp.sum(d_att * out_two, axis=1, keepdims=True)
        grad_probs = dot_nt(d_att_b, v)
        ds_one = (prob_one * (grad_probs - delta_one)).astype(jnp.bfloat16)
        ds_two = (prob_two * (-lam * grad_probs - delta_two)).astype(jnp.bfloat16)
        dq_one = jnp.dot(ds_one, k, preferred_element_type=jnp.float32)
        dq_two = jnp.dot(ds_two, k, preferred_element_type=jnp.float32)
        dq_ref[rows] = (jnp.where(first, dq_one, dq_two) * score_scale).astype(jnp.bfloat16)
        dk_s[:, cols] += dot_tn(q_two, jnp.concatenate([ds_one, ds_two], axis=0))
        dv_s[:, cols] += dot_tn(d_att_b, prob_one_b) - lam * dot_tn(d_att_b, prob_two_b)

    def step(i, carry):
        tiles = scal[2 + first_tile + i]
        for n in range(1, 5):
            pl.when(tiles == n)(functools.partial(tile, i, n))
        return carry

    lax.fori_loop(0, last_tile - first_tile, step, 0)
    if has_prev:
        back_ref[0] = dk_s[:, :SPAN].T.astype(jnp.bfloat16)
        back_ref[1] = dv_s[:, :SPAN].T.astype(jnp.bfloat16)
        dkv_ref[0] = dk_s[:, SPAN:].T
        dkv_ref[1] = dv_s[:, SPAN:].T
    else:
        dkv_ref[0] = dk_s[...].T
        dkv_ref[1] = dv_s[...].T


def attend(name, tiles, scal, lam, gain, ends, recv, prev, deps=()):
    late = isinstance(recv, list)
    blocks = len(recv) if late else recv.shape[0]
    recv = recv if late else [recv]
    first_tile, last_tile = tiles
    queries = (last_tile - first_tile) * TILE
    window = queries + SPAN
    has_prev = prev is not None
    out_shape = [
        jax.ShapeDtypeStruct((queries, HEAD_DIM), jnp.bfloat16),
        jax.ShapeDtypeStruct((2, queries if has_prev else window, HEAD_DIM), jnp.float32),
    ]
    if has_prev:
        out_shape.append(jax.ShapeDtypeStruct((2, SPAN, HEAD_DIM), jnp.bfloat16))
    inputs = [scal, lam, gain, ends, *recv] + ([prev] if has_prev else [])
    body = functools.partial(attend_kernel, first_tile, last_tile, blocks, has_prev, late)
    count = last_tile - first_tile
    return pl.pallas_call(
        spread(body, len(inputs), deps),
        out_shape=out_shape,
        in_specs=[smem_spec] * 2 + [vmem_spec] * (len(inputs) - 2) + [any_spec] * len(deps),
        out_specs=[vmem_spec] * len(out_shape),
        scratch_shapes=[
            pltpu.VMEM((queries, HEAD_DIM), jnp.bfloat16),
            pltpu.VMEM((queries, HEAD_DIM), jnp.bfloat16),
            pltpu.VMEM((window, HEAD_DIM), jnp.bfloat16),
            pltpu.VMEM((window, HEAD_DIM), jnp.bfloat16),
            pltpu.VMEM((HEAD_DIM, window), jnp.float32),
            pltpu.VMEM((HEAD_DIM, window), jnp.float32),
        ],
        compiler_params=pltpu.CompilerParams(vmem_limit_bytes=36 * 2**20),
        cost_estimate=pl.CostEstimate(
            flops=count * 2 * 10**9, bytes_accessed=count * 10**6, transcendentals=count * 3 * 10**5
        ),
        name=name,
    )(*inputs, *deps)


def merge_column_kernel(dq_b, dkv_b, dq_a, dkv_a, dq_c, dkv_c, dq_d, dkv_d, halo_ref, out, dq_s, sum_s):
    dq_s[0:768] = dq_a[...]
    dq_s[768:2048] = dq_b[...]
    dq_s[2048:2304] = dq_c[...]
    dq_s[2304:3072] = dq_d[...]
    for a in range(2):
        sum_s[a, 0:768] = dkv_b[a, 0:768] + dkv_a[a]
        sum_s[a, 768:1280] = dkv_b[a, 768:1280]
        sum_s[a, 1280:1536] = dkv_b[a, 1280:1536] + dkv_c[a, 0:256]
        sum_s[a, 1536:2048] = dkv_b[a, 1536:2048] + dkv_c[a, 256:768] + dkv_d[a, 0:512]
        sum_s[a, 2048:2304] = dkv_c[a, 768:1024] + dkv_d[a, 512:768]
        sum_s[a, 2304:3072] = dkv_d[a, 768:1536] + halo_ref[a].astype(jnp.float32)
    for block in range(COLUMN):
        rows, b = slice(block * ROWS, (block + 1) * ROWS), PLACE[block]
        out[b, 0] = dq_s[rows]
        out[b, 1] = sum_s[0, rows].astype(jnp.bfloat16)
        out[b, 2] = sum_s[1, rows].astype(jnp.bfloat16)


def merge_column(parts, halo, deps=()):
    run = COLUMN * ROWS
    return pl.pallas_call(
        spread(merge_column_kernel, 9, deps),
        out_shape=jax.ShapeDtypeStruct((COLUMN, 3, ROWS, HEAD_DIM), jnp.bfloat16),
        in_specs=[vmem_spec] * 9 + [any_spec] * len(deps),
        out_specs=vmem_spec,
        scratch_shapes=[
            pltpu.VMEM((run, HEAD_DIM), jnp.bfloat16),
            pltpu.VMEM((2, run, HEAD_DIM), jnp.float32),
        ],
        compiler_params=pltpu.CompilerParams(vmem_limit_bytes=24 * 2**20),
        cost_estimate=pl.CostEstimate(flops=0, bytes_accessed=8 * 10**6, transcendentals=0),
        name="merge_column",
    )(*parts, halo, *deps)


def merge_late_kernel(hp_ref, dq_ref, dkv_ref, halo_ref, *outs):
    for k, out in enumerate(outs):
        rows = pl.ds(pl.multiple_of(lax.rem(hp_ref[0] + 4 - k, 4) * ROWS, ROWS), ROWS)
        out[0] = dq_ref[rows]
        for a in range(2):
            out[1 + a] = (dkv_ref[a, rows] + halo_ref[a, rows].astype(jnp.float32)).astype(
                jnp.bfloat16
            )


def merge_late(hp, dq, dkv, halo, deps=()):
    return pl.pallas_call(
        spread(merge_late_kernel, 4, deps),
        out_shape=[jax.ShapeDtypeStruct((3, ROWS, HEAD_DIM), jnp.bfloat16)] * 4,
        in_specs=[smem_spec] + [vmem_spec] * 3 + [any_spec] * len(deps),
        out_specs=[vmem_spec] * 4,
        compiler_params=pltpu.CompilerParams(vmem_limit_bytes=8 * 2**20),
        cost_estimate=pl.CostEstimate(flops=0, bytes_accessed=2 * 10**6, transcendentals=0),
        name="merge_late",
    )(hp, dq, dkv, halo, *deps)


def unpack_kernel(hp_ref, col_ref, l0, l1, l2, l3, *rest):
    outs, sem = rest[:3], rest[3]
    pairs = [
        (col_ref.at[h, a], outs[a].at[:, columns(h)]) for a in range(3) for h in range(COLUMN)
    ]
    for k, src in enumerate((l0, l1, l2, l3)):
        cols = columns(COLUMN + lax.rem(hp_ref[0] + k, 4))
        pairs += [(src.at[a], outs[a].at[:, cols]) for a in range(3)]
    run_copies(pairs, sem)


def unpack(hp, column, late, width):
    return pl.pallas_call(
        unpack_kernel,
        out_shape=[jax.ShapeDtypeStruct((ROWS, width), jnp.bfloat16)] * 3,
        in_specs=[smem_spec] + [any_spec] * 5,
        out_specs=[any_spec] * 3,
        scratch_shapes=[pltpu.SemaphoreType.DMA((60,))],
        compiler_params=pltpu.CompilerParams(vmem_limit_bytes=4 * 2**20),
        name="unpack",
    )(hp, column, *late)


def per_device(queries, keys, values, grad_out, lambdas, norm_gain, doc_lengths):
    col, z_lo, core, hp = (lax.axis_index(a) for a in AXES)
    hp_s = hp[None].astype(jnp.int32)
    doc_ends = jnp.cumsum(doc_lengths)
    ends = doc_ends[None, :]
    gain = norm_gain[None, :]

    def scalars(start, tiles):
        at = start + TILE * jnp.arange(tiles, dtype=jnp.int32)
        begin = jnp.max(jnp.where(ends <= at[:, None], ends, 0), axis=1)
        count = 4 + jnp.arange(tiles, dtype=jnp.int32) - (begin - (start - SPAN)) // TILE
        return jnp.concatenate([hp_s, start[None], count]).astype(jnp.int32)

    column_scal = scalars(col * (COLUMN * ROWS), 12)
    late_scal = scalars((col * 4 + z_lo * 2 + core) * SPAN, 3)
    column_lam = lax.dynamic_slice_in_dim(lambdas, core * 8 + z_lo * 4 + hp, 1)
    late_lam = lax.dynamic_slice_in_dim(lambdas, COLUMN + hp, 1)
    arrays = (keys, values, queries, grad_out)

    chunk = [(d, d + 4) for d in range(252)]
    run = [(d, d + 16) for d in range(240)]
    turn = [[(d, d // 4 * 4 + (d + k) % 4) for d in range(256)] for k in range(4)]

    def back(route):
        return [(b, a) for a, b in route]

    def send(block, route):
        return lax.ppermute(block, AXES, route)

    packed = pack_column(arrays, ())
    recv = lax.all_to_all(packed, RING, split_axis=0, concat_axis=0, tiled=True)
    late_sent = pack_late(hp_s, arrays, (packed,))
    late_recv = [late_sent[0]] + [send(late_sent[k], turn[k]) for k in range(1, 4)]
    prev = send(recv[12:, :2], run)

    b_part = attend("attend_b", (3, 8), column_scal, column_lam, gain, ends, recv, None, (late_sent[0],))
    late_prev = send(late_halo_rows(late_recv, (b_part[0],)), chunk)
    a_part = attend("attend_a", (0, 3), column_scal, column_lam, gain, ends, recv, prev, (b_part[0],))
    halo = send(a_part[2], back(run))
    late_part = attend(
        "attend_late", (0, 3), late_scal, late_lam, gain, ends, late_recv, late_prev, (a_part[0],)
    )
    late_halo = send(late_part[2], back(chunk))
    c_part = attend("attend_c", (8, 9), column_scal, column_lam, gain, ends, recv, None, (late_part[0],))
    late_merged = merge_late(hp_s, late_part[0], late_part[1], late_halo, (c_part[0],))
    late = [late_merged[0]] + [send(late_merged[k], back(turn[k])) for k in range(1, 4)]
    d_part = attend("attend_d", (9, 12), column_scal, column_lam, gain, ends, recv, None, (late_merged[0],))
    merged = merge_column((*b_part, *a_part[:2], *c_part, *d_part), halo, tuple(late[1:]))
    column = lax.all_to_all(merged, RING, split_axis=0, concat_axis=0, tiled=True)
    return tuple(unpack(hp_s, column, late, queries.shape[1]))


def solution(mesh):
    grid = Mesh(mesh.devices.reshape(16, 2, 2, 4), AXES)
    spec = P(AXES, None)
    return jax.shard_map(
        per_device,
        mesh=grid,
        in_specs=(spec,) * 4 + (P(),) * 3,
        out_specs=(spec,) * 3,
        check_vma=False,
    )
```
